512 devices in a mesh: gx: 128 (over y, z, core), gz: 4 (over x).
Axes of the slice: x: 4, y: 8, z: 8, core: 2. Of those that a mesh axis runs over, the one named last changes fastest.
Arguments:
- field: bfloat16 [1024, 8, 32, 1024], P('gx', 'gz'), may hold values from -6 to 6
- cotangent: bfloat16 [1024, 8, 32, 1024], P('gx', 'gz'), may hold values from -6 to 6
- spectral_weight: bfloat16 [8192, 2048], P('gx'), may hold values from -8 to 8
- local_weight: bfloat16 [32, 32], replicated, may hold values from -1 to 1
- bias: float32 [32], replicated, may hold values from -1 to 1
Outputs:
- field_grad: bfloat16 [1024, 8, 32, 1024], P('gx', 'gz')
- spectral_grad: bfloat16 [8192, 2048], P('gx')
- local_grad: float32 [32, 32], replicated
- bias_grad: float32 [32], replicated
The draws below stay inside these ranges and needn't reach their ends.
All inputs are finite; a program needn't handle non-finite values.
Results may differ from the reference program's by a relative error of at most 0.022.
Values may be sent and summed in bfloat16 or wider, within the bound.
No kernel may reach another device: no remote copies, remote signals or barrier semaphores. Data moves between devices by JAX's collectives and lax.ppermute only.
A program may use at most 64 MiB of HBM per device.

```python
import jax
import jax.numpy as jnp
from jax import lax

NY = 1024
C = 32
KX = 128
KY = 64
NX = 1024
NZ = 8
MODES = 8192


def steps_of(own_key, extent, split, smallest, high):
    level = 1.0
    for position, shards_of in split:
        draws = jax.random.uniform(jax.random.fold_in(jax.random.fold_in(own_key, 6), position), (shards_of,), jnp.float32, smallest / len(split), high / len(split))
        level = level * jnp.repeat(jnp.exp(draws), extent[position] // shards_of).reshape((-1,) + (1,) * (len(extent) - 1 - position))
    return level


def bell_draw(stream_key, extent, spread, bound, cuts=(), held_as=jnp.bfloat16):
    drawn = jax.random.normal(stream_key, extent, jnp.float32) * spread
    if len(cuts) > 0:
        drawn = steps_of(stream_key, extent, cuts, -0.22, 0.18) * drawn
    return jnp.clip(drawn, min=-bound, max=bound).astype(held_as)


def setup_inputs(seed: int = 0) -> dict:
    key_list = jax.random.split(jax.random.key(seed), 6)
    field = bell_draw(key_list[0], (NX, NZ, C, NY), 1.0, 6.0, ((0, 128), (1, 4)))
    cotangent = bell_draw(key_list[1], (NX, NZ, C, NY), 1.0, 6.0, ((0, 128), (1, 4)))
    spectral_weight = bell_draw(key_list[2], (MODES, 2 * C * C), 1.4, 8.0, ((0, 128),))
    local_weight = bell_draw(key_list[3], (C, C), C ** -0.5, 1.0)
    bias = jnp.clip(jax.random.uniform(key_list[4], (C,), jnp.float32, -1.0, 1.0), -1.0, 1.0)
    return dict(field=field, cotangent=cotangent, spectral_weight=spectral_weight, local_weight=local_weight, bias=bias)


HIGH = lax.Precision.HIGHEST


def twiddles(freq, pos, length):
    prod_index = (freq[:, None] * pos[None, :]) % length
    angle = prod_index.astype(jnp.float32) * (2.0 * jnp.pi / length)
    return jnp.cos(angle), jnp.sin(angle)


def outer_product_term(form, left, right):
    return jnp.einsum(form, left.astype(jnp.float32), right.astype(jnp.float32), precision=HIGH)


def reference(field, cotangent, spectral_weight, local_weight, bias):
    ky_all = jnp.arange(KY, dtype=jnp.int32)
    ycos, ysin = twiddles(jnp.arange(NY, dtype=jnp.int32), ky_all, NY)
    ytab = jnp.stack([ycos, -ysin], axis=2).reshape(NY, 2 * KY).astype(jnp.bfloat16)
    jall = jnp.arange(KX, dtype=jnp.int32)
    freq = jnp.where(jall < KX // 2, jall, jall - KX)
    xcos, xsin = twiddles(freq, jnp.arange(NX, dtype=jnp.int32), NX)
    xcos = xcos.astype(jnp.bfloat16)
    xsin = xsin.astype(jnp.bfloat16)
    weight_column_vector = jnp.where(ky_all == 0, 1.0, 2.0).astype(jnp.float32)
    ones_col = jnp.ones((KY,), jnp.float32)
    weights = spectral_weight.reshape(KY, KX, 2, C, C)
    weight_real_part = weights[:, :, 0]
    weight_imaginary_part = weights[:, :, 1]
    xscale = NX ** -0.5
    yscale = NY ** -0.5

    def ydft(values):
        spectra = (outer_product_term('xcy,yq->xqc', values, ytab) * yscale).astype(jnp.bfloat16)
        return spectra.reshape(NX, KY, 2, C)

    def xdft(spectra, factor):
        real = spectra[:, :, 0]
        imag = spectra[:, :, 1]
        total_re = outer_product_term('jx,xkc->kjc', xcos, real) + outer_product_term('jx,xkc->kjc', xsin, imag)
        total_im = outer_product_term('jx,xkc->kjc', xcos, imag) - outer_product_term('jx,xkc->kjc', xsin, real)
        scale = (xscale * factor)[:, None, None]
        return (total_re * scale).astype(jnp.bfloat16), (total_im * scale).astype(jnp.bfloat16)

    def xinv(query_real_part, qim):
        back_re = outer_product_term('jx,kjc->xkc', xcos, query_real_part) - outer_product_term('jx,kjc->xkc', xsin, qim)
        back_im = outer_product_term('jx,kjc->xkc', xcos, qim) + outer_product_term('jx,kjc->xkc', xsin, query_real_part)
        joined = (jnp.stack([back_re, back_im], axis=2) * xscale).astype(jnp.bfloat16)
        return joined.reshape(NX, 2 * KY, C)

    def level(carry, inputs):
        acc_local, acc_bias, acc_re, acc_im = carry
        field_z, cot_z = inputs
        first_real_part, first_imaginary_part = xdft(ydft(field_z), ones_col)
        second_real_part = outer_product_term('urh,urhm->urm', first_real_part, weight_real_part) - outer_product_term('urh,urhm->urm', first_imaginary_part, weight_imaginary_part)
        vim = outer_product_term('urh,urhm->urm', first_real_part, weight_imaginary_part) + outer_product_term('urh,urhm->urm', first_imaginary_part, weight_real_part)
        query_real_part = (second_real_part * weight_column_vector[:, None, None]).astype(jnp.bfloat16)
        qim = (vim * weight_column_vector[:, None, None]).astype(jnp.bfloat16)
        spec = outer_product_term('xqc,yq->xcy', xinv(query_real_part, qim), ytab) * yscale
        pre = spec + outer_product_term('xiy,io->xoy', field_z, local_weight) + bias[None, :, None]
        sig = jax.nn.sigmoid(pre)
        delta = (cot_z.astype(jnp.float32) * (sig * (1.0 + pre * (1.0 - sig)))).astype(jnp.bfloat16)
        acc_local = acc_local + outer_product_term('xiy,xoy->io', field_z, delta)
        acc_bias = acc_bias + jnp.sum(delta.astype(jnp.float32), axis=(0, 2))
        dre, dim = xdft(ydft(delta), weight_column_vector)
        acc_re = acc_re + outer_product_term('kji,kjo->kjio', first_real_part, dre) + outer_product_term('kji,kjo->kjio', first_imaginary_part, dim)
        acc_im = acc_im + outer_product_term('kji,kjo->kjio', first_real_part, dim) - outer_product_term('kji,kjo->kjio', first_imaginary_part, dre)
        gre = (outer_product_term('kjo,kjio->kji', dre, weight_real_part) + outer_product_term('kjo,kjio->kji', dim, weight_imaginary_part)).astype(jnp.bfloat16)
        gim = (outer_product_term('kjo,kjio->kji', dim, weight_real_part) - outer_product_term('kjo,kjio->kji', dre, weight_imaginary_part)).astype(jnp.bfloat16)
        grad_z = outer_product_term('xqc,yq->xcy', xinv(gre, gim), ytab) * yscale
        grad_z = (grad_z + outer_product_term('xoy,io->xiy', delta, local_weight)).astype(jnp.bfloat16)
        return (acc_local, acc_bias, acc_re, acc_im), grad_z

    start = (jnp.zeros((C, C), jnp.float32), jnp.zeros((C,), jnp.float32),
             jnp.zeros((KY, KX, C, C), jnp.float32), jnp.zeros((KY, KX, C, C), jnp.float32))
    carry, grads = lax.scan(level, start, (jnp.transpose(field, (1, 0, 2, 3)), jnp.transpose(cotangent, (1, 0, 2, 3))))
    acc_local, acc_bias, acc_re, acc_im = carry
    gscale = (NX * NY * NZ) ** -0.5
    field_grad = jnp.transpose(grads, (1, 0, 2, 3))
    spectral_grad = jnp.stack([acc_re, acc_im], axis=2).reshape(MODES, 2 * C * C).astype(jnp.bfloat16)
    return field_grad, spectral_grad, acc_local * gscale, acc_bias * gscale
```

```python
import jax
import jax.numpy as jnp
import ml_dtypes
import numpy as np
from jax import lax
from jax.experimental import pallas as pl
from jax.experimental.pallas import tpu as pltpu
from jax.sharding import Mesh
from jax.sharding import PartitionSpec as P

KX = 128
KY = 64
C = 32
N = 1024
F32 = jnp.float32
BF16 = jnp.bfloat16
GX = ("y", "zh", "zl", "core")
VM = pl.BlockSpec(memory_space=pltpu.VMEM)


def angles(freq, pos):
    product = (freq[:, None].astype(np.int64) * pos[None, :].astype(np.int64)) % N
    angle = product.astype(np.float32) * np.float32(2.0 * np.pi / N)
    return np.cos(angle).astype(np.float32), np.sin(angle).astype(np.float32)


def tables():
    ycos, ysin = angles(np.arange(KY), np.arange(N))
    ytab = np.concatenate([ycos, -ysin], axis=0).astype(ml_dtypes.bfloat16)
    ytab = (ytab.astype(np.float32) / 32.0).astype(ml_dtypes.bfloat16)
    j = np.arange(KX)
    freq = np.where(j < KX // 2, j, j - KX)
    r, h, d = np.meshgrid(np.arange(4), np.arange(2), np.arange(128), indexing="ij")
    xcos, xsin = angles(freq, (8 * d + 4 * h + r).reshape(-1))
    forward = np.concatenate([xcos, xsin], axis=0).astype(ml_dtypes.bfloat16)
    inverse = forward.reshape(2 * KX, 4, 256).transpose(2, 1, 0).reshape(256, 1024)
    return ytab, forward, np.ascontiguousarray(inverse)


def nt(a, b):
    return lax.dot_general(a, b, (((1,), (1,)), ((), ())), preferred_element_type=F32)


def nn(a, b):
    return jnp.dot(a, b, preferred_element_type=F32)


def block_of(shape):
    return (lax.broadcasted_iota(jnp.int32, shape, 1) >> 5) & 3


def fold(v):
    v = v + pltpu.roll(v, 64, 1)
    return v + pltpu.roll(v, 32, 1)


def spread(base):
    block = block_of(base.shape)
    return jnp.concatenate([jnp.where(block == r, base, 0.0) for r in range(4)], axis=0).astype(BF16)


def rounded(v):
    return v.astype(BF16).astype(F32)


def mode_weight():
    first = (lax.axis_index("y") + lax.axis_index("zh") + lax.axis_index("zl")) == 0
    return jnp.where(first, 1.0, 2.0).astype(F32)


def x_forward(recv, table, held):
    held[...] = recv[...].astype(F32)
    parts = [
        jnp.concatenate([held[pl.ds(2 * p + h, 128, stride=4), :] for h in range(2)], axis=0)
        for p in range(2)
    ]
    out = nn(table[...], spread(jnp.concatenate(parts, axis=1)))
    real = out[:KX, :128] + out[KX:, 128:]
    imag = out[:KX, 128:] - out[KX:, :128]
    return fold(real) * (1.0 / 32.0), fold(imag) * (1.0 / 32.0)


def x_inverse(real, imag, table, held, stride):
    base = jnp.concatenate(
        [jnp.concatenate([real, imag], axis=1), jnp.concatenate([-imag, real], axis=1)], axis=0
    )
    out = nn(table[...], spread(base)) * (1.0 / 32.0)
    for p in range(2):
        for h in range(2):
            held[pl.ds(2 * p + h, 128, stride=stride), :] = out[
                128 * h : 128 * (h + 1), 128 * p : 128 * (p + 1)
            ]


def y_kernel(field, ytab, send, held):
    for z in range(2):
        for h in range(2):
            rows = field[4 * h : 4 * h + 4, z].reshape(128, N)
            out = nt(ytab[...], rows)
            for p in range(2):
                held[pl.ds(4 * z + 2 * p + h, KY, stride=8), :] = out[KY * p : KY * (p + 1)]
    send[...] = held[...].astype(BF16)


def mix_kernel(recv, weight, forward, inverse, send, kept, held):
    real, imag = x_forward(recv, forward, held)
    real = rounded(real)
    imag = rounded(imag)
    kept[:KX] = real
    kept[KX:] = imag
    k = lax.broadcasted_iota(jnp.int32, (128, 1024), 0)
    lane = lax.broadcasted_iota(jnp.int32, (128, 1024), 1)
    expand = jnp.where((lane >> 5) == k, 1.0, 0.0).astype(BF16)
    wide = nn(jnp.concatenate([real, imag], axis=0).astype(BF16), expand)
    vre = jnp.zeros((KX, 128), F32)
    vim = jnp.zeros((KX, 128), F32)
    for t in range(8):
        wre = weight[:, 128 * t : 128 * (t + 1)].astype(F32)
        wim = weight[:, 1024 + 128 * t : 1024 + 128 * (t + 1)].astype(F32)
        ure = wide[:KX, 128 * t : 128 * (t + 1)]
        uim = wide[KX:, 128 * t : 128 * (t + 1)]
        vre = vre + (ure * wre - uim * wim)
        vim = vim + (ure * wim + uim * wre)
    factor = mode_weight()
    x_inverse(rounded(fold(vre) * factor), rounded(fold(vim) * factor), inverse, held, 4)
    send[...] = held[...].astype(BF16)


def point_kernel(recv, field, cotangent, local4, bias4, ytab, send, delta, sums, held):
    held[...] = recv[...].astype(F32)
    ones = jnp.ones((16, N), BF16)
    total = jnp.zeros((128, 128), F32)
    bias_total = jnp.zeros((16, 128), F32)
    outs = []
    for z in range(2):
        for h in range(2):
            spectrum = jnp.concatenate(
                [held[pl.ds(4 * z + 2 * p + h, KY, stride=8), :] for p in range(2)], axis=0
            )
            left = jnp.concatenate([spectrum.T.astype(BF16), local4[...]], axis=1)
            rows = field[4 * h : 4 * h + 4, z].reshape(128, N)
            cot = cotangent[4 * h : 4 * h + 4, z].reshape(128, N)
            for part in range(4):
                cols = slice(256 * part, 256 * (part + 1))
                right = jnp.concatenate([ytab[:, cols], rows[:, cols]], axis=0)
                pre = nn(left, right) + bias4[...]
                sig = 0.5 * jnp.tanh(0.5 * pre) + 0.5
                slope = sig * (1.0 + pre * (1.0 - sig))
                delta[2 * z + h, :, cols] = (cot[:, cols].astype(F32) * slope).astype(BF16)
            grad = delta[2 * z + h]
            outs.append((z, h, nt(ytab[...], grad)))
            total = total + nt(rows, grad)
            bias_total = bias_total + nt(ones, grad)
    for z, h, out in outs:
        for p in range(2):
            held[pl.ds(4 * z + 2 * p + h, KY, stride=8), :] = out[KY * p : KY * (p + 1)]
    send[...] = held[...].astype(BF16)
    block = block_of((32, 128))
    diag = jnp.zeros((32, 128), F32)
    for r in range(4):
        diag = diag + jnp.where(block == r, total[32 * r : 32 * (r + 1)], 0.0)
    held[0:32, :] = fold(diag)
    block = block_of((8, 128))
    flat = jnp.zeros((8, 128), F32)
    for q in range(4):
        flat = flat + jnp.where(block == q, held[pl.ds(q, 8, stride=4), :], 0.0)
    sums[0:8, :] = flat
    sums[8:16, :] = fold(bias_total[0:8])
    sums[16:, :] = jnp.zeros((112, 128), F32)


def back_kernel(recv, forward, kept, held):
    real, imag = x_forward(recv, forward, held)
    factor = mode_weight()
    kept[:KX] = rounded(real * factor)
    kept[KX:] = rounded(imag * factor)


def adjoint_kernel(kept, weight, inverse, gathered, send, held, high, low):
    dre = kept[:KX]
    dim = kept[KX:]
    for t in range(8):
        cols = slice(128 * t, 128 * (t + 1))
        wre = weight[:, cols].astype(F32)
        wim = weight[:, 1024 + 128 * t : 1024 + 128 * (t + 1)].astype(F32)
        for k, term in ((0, dre * wre + dim * wim), (1, dim * wre - dre * wim)):
            top = term.astype(BF16)
            high[KX * k : KX * (k + 1), cols] = top
            low[KX * k : KX * (k + 1), cols] = (term - top.astype(F32)).astype(BF16)
    k = lax.broadcasted_iota(jnp.int32, (1024, 128), 0)
    lane = lax.broadcasted_iota(jnp.int32, (1024, 128), 1)
    gather = jnp.where((k >> 5) == (lane & 31), 1.0, 0.0).astype(BF16)
    back = rounded(nn(high[...], gather) + nn(low[...], gather))
    x_inverse(back[:KX], back[KX:], inverse, held, 8)
    quarter = 2 * lax.axis_index("zl") + lax.axis_index("core")
    summed = gathered[0:16, :]
    for k in range(1, 16):
        summed = summed + gathered[128 * k : 128 * k + 16, :]
    own = jnp.zeros((2, 128), F32)
    for q in range(4):
        own = own + jnp.where(quarter == q, summed[2 * q : 2 * q + 2], 0.0)
    first = rounded(own)
    second = rounded(own - first)
    bias = summed[8:9]
    bias_1 = rounded(bias)
    bias_2 = rounded(bias - bias_1)
    bias_3 = rounded(bias - bias_1 - bias_2)
    piece = jnp.where(
        quarter == 0, bias_1, jnp.where(quarter == 1, bias_2, jnp.where(quarter == 2, bias_3, 0.0))
    )
    last = jnp.where(block_of((1, 128)) == 3, piece, second[1:2])
    for k, row in enumerate((first[0:1], first[1:2], second[0:1], last)):
        held[pl.ds(4 + k, 128, stride=8), :] = jnp.broadcast_to(row, (128, 128))
    send[...] = held[...].astype(BF16)


def grad_kernel(recv, delta, local4, ytab, field_grad, local_grad, bias_grad, held):
    held[...] = recv[...].astype(F32)
    for z in range(2):
        for h in range(2):
            spectrum = jnp.concatenate(
                [held[pl.ds(8 * z + 2 * p + h, KY, stride=16), :] for p in range(2)], axis=0
            )
            left = jnp.concatenate([spectrum.T.astype(BF16), local4[...]], axis=1)
            for part in range(4):
                cols = slice(256 * part, 256 * (part + 1))
                right = jnp.concatenate([ytab[:, cols], delta[2 * z + h, :, cols]], axis=0)
                field_grad[4 * h : 4 * h + 4, z, :, cols] = (
                    nn(left, right).astype(BF16).reshape(4, 32, 256)
                )
    gscale = float((N * N * 8) ** -0.5)
    block = block_of((1, 128))
    rows = []
    bias = jnp.zeros((1, 128), F32)
    for q in range(4):
        took = [
            jnp.sum(held[pl.ds(8 * q + 4 + k, 32, stride=32), :], axis=0, keepdims=True)
            for k in range(4)
        ]
        bias = bias + jnp.where(block == 3, took[3], 0.0)
        rows.append(took[0] + took[2])
        rows.append(took[1] + jnp.where(block == 3, 0.0, took[3]))
    flat = jnp.concatenate(rows, axis=0) * gscale
    for q in range(4):
        local_grad[pl.ds(q, 8, stride=4), :] = flat[:, 32 * q : 32 * (q + 1)]
    bias_grad[...] = fold(bias)[:, :32] * gscale


def outer_kernel(first, second, out):
    start = 64 * lax.axis_index("core")
    k = lax.broadcasted_iota(jnp.int32, (128, 1024), 0)
    lane = lax.broadcasted_iota(jnp.int32, (128, 1024), 1)
    expand = jnp.where((lane >> 5) == k, 1.0, 0.0).astype(BF16)
    picks = [pl.ds(pl.multiple_of(KX * k + start, 64), 64) for k in range(16)]
    compact = jnp.concatenate([first[pick, :] for pick in picks], axis=0).astype(BF16)
    for pair in range(4):
        wide = nn(compact, expand[:, 256 * pair : 256 * (pair + 1)])
        for half in range(2):
            t = 2 * pair + half
            real = jnp.zeros((64, 128), F32)
            imag = jnp.zeros((64, 128), F32)
            for level in range(8):
                ure = wide[128 * level : 128 * level + 64, 128 * half : 128 * (half + 1)]
                uim = wide[128 * level + 64 : 128 * level + 128, 128 * half : 128 * (half + 1)]
                dre = second[picks[2 * level], :]
                dim = second[picks[2 * level + 1], :]
                real = real + (ure * dre + uim * dim)
                imag = imag + (ure * dim - uim * dre)
            out[:, 128 * t : 128 * (t + 1)] = real.astype(BF16)
            out[:, 1024 + 128 * t : 1024 + 128 * (t + 1)] = imag.astype(BF16)


def run(kernel, operands, outs, scratch, name, flops=200_000_000):
    shapes = [jax.ShapeDtypeStruct(shape, dtype) for shape, dtype in outs]
    return pl.pallas_call(
        kernel,
        out_shape=shapes,
        in_specs=[VM] * len(operands),
        out_specs=[VM] * len(shapes),
        scratch_shapes=[pltpu.VMEM(shape, dtype) for shape, dtype in scratch],
        compiler_params=pltpu.CompilerParams(vmem_limit_bytes=24 * 1024 * 1024),
        cost_estimate=pl.CostEstimate(flops=flops, bytes_accessed=1 << 20, transcendentals=0),
        name=name,
    )(*operands)


def exchange(values, rows):
    blocks = values.reshape(128, rows, 128)
    return lax.all_to_all(blocks, GX, 0, 0, tiled=True).reshape(128 * rows, 128)


def local(field, cotangent, spectral_weight, local_weight, bias):
    ytab, forward, inverse = (jnp.asarray(table) for table in tables())
    same = jnp.asarray(np.kron(np.eye(4), np.ones((C, C))).astype(ml_dtypes.bfloat16))
    local_in = jnp.tile(local_weight, (4, 4)) * same
    local_out = jnp.tile(local_weight.T, (4, 4)) * same
    bias4 = jnp.tile(bias, 4)[:, None]
    slab = ((512, 128), BF16)
    held = ((512, 128), F32)
    kept = ((256, 128), F32)

    (send,) = run(y_kernel, (field, ytab), [slab], [held], "y_forward")
    recv = exchange(send, 4)
    weight = lax.all_gather(spectral_weight, "core", axis=0, tiled=True)
    send, first = run(
        mix_kernel, (recv, weight, forward, inverse), [slab, kept], [held], "mix"
    )
    first_all = lax.all_gather(first, ("core", "gz"), axis=0, tiled=True)
    recv = exchange(send, 4)
    send, delta, sums = run(
        point_kernel,
        (recv, field, cotangent, local_out, bias4, ytab),
        [slab, ((4, 128, N), BF16), ((128, 128), F32)],
        [held],
        "pointwise",
    )
    sums_all = lax.all_gather(sums, ("zl", "core", "gz"), axis=0, tiled=True)
    recv = exchange(send, 4)
    (second,) = run(back_kernel, (recv, forward), [kept], [held], "x_forward")
    second_all = lax.all_gather(second, ("core", "gz"), axis=0, tiled=True)
    (send,) = run(
        adjoint_kernel,
        (second, weight, inverse, sums_all),
        [((1024, 128), BF16)],
        [((1024, 128), F32), ((256, 1024), BF16), ((256, 1024), BF16)],
        "adjoint",
    )
    recv = exchange(send, 8)
    field_grad, local_grad, bias_grad = run(
        grad_kernel,
        (recv, delta, local_in, ytab),
        [((8, 2, C, N), BF16), ((C, C), F32), ((1, C), F32)],
        [((1024, 128), F32)],
        "y_inverse",
    )
    (spectral_grad,) = run(
        outer_kernel, (first_all, second_all), [((64, 2048), BF16)], [], "outer"
    )
    return field_grad, spectral_grad, local_grad, bias_grad.reshape(C)


def solution(mesh):
    fine = Mesh(mesh.devices.reshape(8, 4, 2, 2, 4), GX + ("gz",))
    cells = P(GX, "gz", None, None)
    return jax.shard_map(
        local,
        mesh=fine,
        in_specs=(cells, cells, P(GX, None), P(), P()),
        out_specs=(cells, P(GX, None), P(), P()),
        check_vma=False,
    )
```

```python
import jax
import jax.numpy as jnp
import ml_dtypes
import numpy as np
from jax import lax
from jax.experimental import pallas as pl
from jax.experimental.pallas import tpu as pltpu
from jax.sharding import Mesh
from jax.sharding import PartitionSpec as P

KX = 128
KY = 64
C = 32
N = 1024
F32 = jnp.float32
BF16 = jnp.bfloat16
GX = ("y", "z", "core")
VM = pl.BlockSpec(memory_space=pltpu.VMEM)
ANY = pl.BlockSpec(memory_space=pl.ANY)


def angles(freq, pos):
    product = (freq[:, None].astype(np.int64) * pos[None, :].astype(np.int64)) % N
    angle = product.astype(np.float32) * np.float32(2.0 * np.pi / N)
    return np.cos(angle).astype(np.float32), np.sin(angle).astype(np.float32)


def tables():
    ycos, ysin = angles(np.arange(KY), np.arange(N))
    ytab = np.concatenate([ycos, -ysin], axis=0).astype(ml_dtypes.bfloat16)
    ytab = (ytab.astype(np.float32) / 32.0).astype(ml_dtypes.bfloat16)
    j = np.arange(KX)
    freq = np.where(j < KX // 2, j, j - KX)
    r, h, d = np.meshgrid(np.arange(4), np.arange(2), np.arange(128), indexing="ij")
    xcos, xsin = angles(freq, (8 * d + 4 * h + r).reshape(-1))
    forward = np.concatenate([xcos, xsin], axis=0).astype(ml_dtypes.bfloat16)
    inverse = forward.reshape(2 * KX, 4, 256).transpose(2, 1, 0).reshape(256, 1024)
    return ytab, forward, np.ascontiguousarray(inverse)


def nt(a, b):
    return lax.dot_general(a, b, (((1,), (1,)), ((), ())), preferred_element_type=F32)


def nn(a, b):
    return jnp.dot(a, b, preferred_element_type=F32)


def block_of(shape):
    return (lax.broadcasted_iota(jnp.int32, shape, 1) >> 5) & 3


def fold(v):
    v = v + pltpu.roll(v, 64, 1)
    return v + pltpu.roll(v, 32, 1)


def spread(base):
    block = block_of(base.shape)
    return jnp.concatenate([jnp.where(block == r, base, 0.0) for r in range(4)], axis=0).astype(BF16)


def rounded(v):
    return v.astype(BF16).astype(F32)


def mode_weight():
    first = (lax.axis_index("y") + lax.axis_index("z")) == 0
    return jnp.where(first, 1.0, 2.0).astype(F32)


def x_forward(recv, table, held, stride):
    held[...] = recv[...].astype(F32)
    parts = [
        jnp.concatenate([held[pl.ds(2 * p + h, 128, stride=stride), :] for h in range(2)], axis=0)
        for p in range(2)
    ]
    out = nn(table[...], spread(jnp.concatenate(parts, axis=1)))
    real = out[:KX, :128] + out[KX:, 128:]
    imag = out[:KX, 128:] - out[KX:, :128]
    return fold(real) * (1.0 / 32.0), fold(imag) * (1.0 / 32.0)


def paired(real, imag):
    return jnp.where((block_of(real.shape) & 1) == 0, real, imag)


def x_inverse(real, imag, table, held, stride):
    base = jnp.concatenate(
        [jnp.concatenate([real, imag], axis=1), jnp.concatenate([-imag, real], axis=1)], axis=0
    )
    out = nn(table[...], spread(base)) * (1.0 / 32.0)
    for p in range(2):
        for h in range(2):
            held[pl.ds(2 * p + h, 128, stride=stride), :] = out[
                128 * h : 128 * (h + 1), 128 * p : 128 * (p + 1)
            ]


def y_kernel(field, ytab, send, held, rows, table, sems):
    copies = [pltpu.make_async_copy(ytab, table, sems.at[4])]
    for k in range(4):
        part = field.at[pl.ds(4 * (k % 2), 4), k // 2]
        copies.append(pltpu.make_async_copy(part, rows.at[k], sems.at[k]))
    for copy in copies:
        copy.start()
    copies[0].wait()
    for k in range(4):
        z, h = k // 2, k % 2
        copies[1 + k].wait()
        out = nt(table[...], rows[k].reshape(128, N))
        for p in range(2):
            held[pl.ds(4 * z + 2 * p + h, KY, stride=8), :] = out[KY * p : KY * (p + 1)]
    send[...] = held[...].astype(BF16)


def mix_kernel(recv, weight, forward, inverse, send, kept, held):
    real, imag = x_forward(recv, forward, held, 4)
    real = rounded(real)
    imag = rounded(imag)
    kept[...] = paired(real, imag).astype(BF16)
    k = lax.broadcasted_iota(jnp.int32, (128, 1024), 0)
    lane = lax.broadcasted_iota(jnp.int32, (128, 1024), 1)
    expand = jnp.where((lane >> 5) == k, 1.0, 0.0).astype(BF16)
    wide = nn(jnp.concatenate([real, imag], axis=0).astype(BF16), expand)
    vre = jnp.zeros((KX, 128), F32)
    vim = jnp.zeros((KX, 128), F32)
    for t in range(8):
        wre = weight[:, 128 * t : 128 * (t + 1)].astype(F32)
        wim = weight[:, 1024 + 128 * t : 1024 + 128 * (t + 1)].astype(F32)
        ure = wide[:KX, 128 * t : 128 * (t + 1)]
        uim = wide[KX:, 128 * t : 128 * (t + 1)]
        vre = vre + (ure * wre - uim * wim)
        vim = vim + (ure * wim + uim * wre)
    factor = mode_weight()
    x_inverse(rounded(fold(vre) * factor), rounded(fold(vim) * factor), inverse, held, 4)
    send[...] = held[...].astype(BF16)


def point_kernel(recv, field, cotangent, local4, bias4, ytab, send, delta, held, wide):
    held[...] = recv[...].astype(F32)
    ones = jnp.ones((16, N), BF16)
    total = jnp.zeros((128, 128), F32)
    bias_total = jnp.zeros((16, 128), F32)
    outs = []
    for z in range(2):
        for h in range(2):
            spectrum = jnp.concatenate(
                [held[pl.ds(4 * z + 2 * p + h, KY, stride=8), :] for p in range(2)], axis=0
            )
            left = jnp.concatenate([spectrum.T.astype(BF16), local4[...]], axis=1)
            rows = field[4 * h : 4 * h + 4, z].reshape(128, N)
            cot = cotangent[4 * h : 4 * h + 4, z].reshape(128, N)
            for part in range(4):
                cols = slice(256 * part, 256 * (part + 1))
                right = jnp.concatenate([ytab[:, cols], rows[:, cols]], axis=0)
                pre = nn(left, right) + bias4[...]
                sig = 0.5 * jnp.tanh(0.5 * pre) + 0.5
                slope = sig * (1.0 + pre * (1.0 - sig))
                delta[2 * z + h, :, cols] = (cot[:, cols].astype(F32) * slope).astype(BF16)
            grad = delta[2 * z + h]
            outs.append((z, h, nt(ytab[...], grad)))
            total = total + nt(rows, grad)
            bias_total = bias_total + nt(ones, grad)
    block = block_of((32, 128))
    diag = jnp.zeros((32, 128), F32)
    for r in range(4):
        diag = diag + jnp.where(block == r, total[32 * r : 32 * (r + 1)], 0.0)
    held[0:32, :] = fold(diag)
    block = block_of((8, 128))
    flat = jnp.zeros((8, 128), F32)
    for q in range(4):
        flat = flat + jnp.where(block == q, held[pl.ds(q, 8, stride=4), :], 0.0)
    bias = fold(bias_total[0:8])[0:1]
    bias_1 = rounded(bias)
    bias_2 = rounded(bias - bias_1)
    bias_3 = bias - bias_1 - bias_2
    block = block_of((1, 128))
    pieces = jnp.where(
        block == 0, bias_1, jnp.where(block == 1, bias_2, jnp.where(block == 2, bias_3, 0.0))
    )
    for z, h, out in outs:
        for p in range(2):
            wide[pl.ds(10 * z + 2 * p + h, KY, stride=20), :] = out[KY * p : KY * (p + 1)]
    for z in range(2):
        lines = [flat[4 * z + k : 4 * z + k + 1] for k in range(4)]
        lines = lines + [pieces, jnp.zeros((1, 128), F32)]
        for k, line in enumerate(lines):
            wide[pl.ds(10 * z + 4 + k, KY, stride=20), :] = jnp.broadcast_to(line, (KY, 128))
    send[...] = wide[...].astype(BF16)


def back_kernel(recv, forward, kept, share, held):
    real, imag = x_forward(recv, forward, held, 10)
    factor = mode_weight()
    real = rounded(real * factor)
    imag = rounded(imag * factor)
    kept[:KX] = real
    kept[KX:] = imag
    share[:KX] = paired(real, imag).astype(BF16)
    lines = [
        jnp.sum(held[pl.ds(4 + k, 128, stride=10), :], axis=0, keepdims=True) for k in range(5)
    ]
    total = jnp.concatenate(lines[:4], axis=0)
    bias = fold(lines[4])
    share[KX:] = jnp.concatenate(
        [
            rounded(total),
            total - rounded(total),
            rounded(bias),
            bias - rounded(bias),
            jnp.zeros((6, 128), F32),
        ],
        axis=0,
    ).astype(BF16)


def adjoint_kernel(kept, weight, inverse, firsts, seconds, send, group, held, high, low):
    dre = kept[:KX]
    dim = kept[KX:]
    for t in range(8):
        cols = slice(128 * t, 128 * (t + 1))
        wre = weight[:, cols].astype(F32)
        wim = weight[:, 1024 + 128 * t : 1024 + 128 * (t + 1)].astype(F32)
        for k, term in ((0, dre * wre + dim * wim), (1, dim * wre - dre * wim)):
            top = term.astype(BF16)
            high[KX * k : KX * (k + 1), cols] = top
            low[KX * k : KX * (k + 1), cols] = (term - top.astype(F32)).astype(BF16)
    k = lax.broadcasted_iota(jnp.int32, (1024, 128), 0)
    lane = lax.broadcasted_iota(jnp.int32, (1024, 128), 1)
    gather = jnp.where((k >> 5) == (lane & 31), 1.0, 0.0).astype(BF16)
    back = rounded(nn(high[...], gather) + nn(low[...], gather))
    x_inverse(back[:KX], back[KX:], inverse, held, 4)
    send[...] = held[...].astype(BF16)
    start = 64 * lax.axis_index("core")
    left = block_of((64, 128)) < 2
    for k, (both, step) in enumerate(((firsts, KX), (seconds, KX + 16))):
        one = both[pl.ds(pl.multiple_of(start, 16), 64), :].astype(F32)
        two = both[pl.ds(pl.multiple_of(step + start, 16), 64), :].astype(F32)
        group[64 * k : 64 * (k + 1)] = jnp.where(left, one, two).astype(BF16)
    group[128:144] = seconds[KX : KX + 16]
    group[144:160] = seconds[2 * KX + 16 : 2 * KX + 32]


def grad_kernel(recv, delta, local4, ytab, field_grad, held, rows, sems):
    held[...] = recv[...].astype(F32)
    copies = []
    for k in range(4):
        z, h = k // 2, k % 2
        spectrum = jnp.concatenate(
            [held[pl.ds(4 * z + 2 * p + h, KY, stride=8), :] for p in range(2)], axis=0
        )
        left = jnp.concatenate([spectrum.T.astype(BF16), local4[...]], axis=1)
        for part in range(4):
            cols = slice(256 * part, 256 * (part + 1))
            right = jnp.concatenate([ytab[:, cols], delta[k, :, cols]], axis=0)
            rows[k, :, :, cols] = nn(left, right).astype(BF16).reshape(4, 32, 256)
        copies.append(
            pltpu.make_async_copy(rows.at[k], field_grad.at[pl.ds(4 * h, 4), z], sems.at[k])
        )
        copies[k].start()
    for copy in copies:
        copy.wait()


def outer_kernel(groups, out, local_grad, bias_grad, tiles):
    lane = lax.broadcasted_iota(jnp.int32, (128, 1024), 1)
    k = lax.broadcasted_iota(jnp.int32, (128, 1024), 0)
    expand = jnp.where((lane >> 5) == k, 1.0, 0.0).astype(BF16)
    first = jnp.concatenate([groups[160 * g : 160 * g + 64] for g in range(4)], axis=0).astype(F32)
    turned = [first] + [pltpu.roll(first, 128 - 32 * b, 1) for b in range(1, 4)]
    compact = jnp.concatenate(turned, axis=0).astype(BF16)
    block = block_of((64, 128))
    for g in range(4):
        second = groups[160 * g + 64 : 160 * g + 128].astype(F32)
        for b in range(4):
            tiles[64 * (4 * g + b) : 64 * (4 * g + b + 1)] = fold(
                jnp.where(block == b, second, 0.0)
            )
    for pair in range(4):
        wide = nn(compact, expand[:, 256 * pair : 256 * (pair + 1)])
        for half in range(2):
            t = 2 * pair + half
            cols = slice(128 * half, 128 * (half + 1))
            real = jnp.zeros((64, 128), F32)
            imag = jnp.zeros((64, 128), F32)
            for g in range(4):
                for z in range(2):
                    b = 2 * z
                    ure = wide[256 * b + 64 * g : 256 * b + 64 * (g + 1), cols]
                    uim = wide[256 * (b + 1) + 64 * g : 256 * (b + 1) + 64 * (g + 1), cols]
                    dre = tiles[64 * (4 * g + b) : 64 * (4 * g + b + 1)]
                    dim = tiles[64 * (4 * g + b + 1) : 64 * (4 * g + b + 2)]
                    real = real + (ure * dre + uim * dim)
                    imag = imag + (ure * dim - uim * dre)
            out[:, 128 * t : 128 * (t + 1)] = real.astype(BF16)
            out[:, 1024 + 128 * t : 1024 + 128 * (t + 1)] = imag.astype(BF16)
    gscale = float((N * N * 8) ** -0.5)
    total = groups[128:160].astype(F32)
    for g in range(1, 4):
        total = total + groups[160 * g + 128 : 160 * g + 160].astype(F32)
    flat = jnp.concatenate(
        [total[0:4] + total[4:8], total[16:20] + total[20:24]], axis=0
    ) * gscale
    for q in range(4):
        local_grad[pl.ds(q, 8, stride=4), :] = flat[:, 32 * q : 32 * (q + 1)]
    bias_grad[...] = ((total[8:9] + total[9:10]) * gscale)[:, :32]


def run(kernel, operands, outs, scratch, name, specs=None, out_specs=None):
    shapes = [jax.ShapeDtypeStruct(shape, dtype) for shape, dtype in outs]
    return pl.pallas_call(
        kernel,
        out_shape=shapes,
        in_specs=specs or [VM] * len(operands),
        out_specs=out_specs or [VM] * len(shapes),
        scratch_shapes=scratch,
        compiler_params=pltpu.CompilerParams(vmem_limit_bytes=16 * 1024 * 1024),
        cost_estimate=pl.CostEstimate(
            flops=200_000_000, bytes_accessed=1 << 20, transcendentals=0
        ),
        name=name,
    )(*operands)


def exchange(values, *shape):
    blocks = values.reshape((128,) + shape)
    return lax.all_to_all(blocks, GX, 0, 0, tiled=True).reshape(values.shape)


def local(field, cotangent, spectral_weight, local_weight, bias):
    ytab, forward, inverse = (jnp.asarray(table) for table in tables())
    same = jnp.asarray(np.kron(np.eye(4), np.ones((C, C))).astype(ml_dtypes.bfloat16))
    local_in = jnp.tile(local_weight, (4, 4)) * same
    local_out = jnp.tile(local_weight.T, (4, 4)) * same
    bias4 = jnp.tile(bias, 4)[:, None]
    slab = ((512, 128), BF16)
    slab_wide = ((1280, 128), BF16)
    held = pltpu.VMEM((512, 128), F32)
    held_wide = pltpu.VMEM((1280, 128), F32)
    quarters = pltpu.VMEM((4, 4, C, N), BF16)

    (send,) = run(
        y_kernel,
        (field, ytab),
        [slab],
        [held, quarters, pltpu.VMEM((128, N), BF16), pltpu.SemaphoreType.DMA((5,))],
        "y_forward",
        [ANY, ANY],
    )
    recv = exchange(send, 4, 128)
    weight = lax.all_gather(spectral_weight, "core", axis=0, tiled=True)
    send, first = run(
        mix_kernel,
        (recv, weight, forward, inverse),
        [slab, ((KX, 128), BF16)],
        [held],
        "mix",
    )
    recv = exchange(send, 4, 128)
    firsts = lax.all_gather(first, "core", axis=0, tiled=True)
    send, delta = run(
        point_kernel,
        (recv, field, cotangent, local_out, bias4, ytab),
        [slab_wide, ((4, 128, N), BF16)],
        [held, held_wide],
        "pointwise",
    )
    recv = exchange(send, 5, 2, 128)
    second, share = run(
        back_kernel,
        (recv, forward),
        [((2 * KX, 128), F32), ((KX + 16, 128), BF16)],
        [held_wide],
        "x_forward",
    )
    seconds = lax.all_gather(share, "core", axis=0, tiled=True)
    send, group = run(
        adjoint_kernel,
        (second, weight, inverse, firsts, seconds),
        [slab, ((160, 128), BF16)],
        [held, pltpu.VMEM((256, 1024), BF16), pltpu.VMEM((256, 1024), BF16)],
        "adjoint",
    )
    recv = exchange(send, 4, 128)
    groups = lax.all_gather(group, "gz", axis=0, tiled=True)
    (field_grad,) = run(
        grad_kernel,
        (recv, delta, local_in, ytab),
        [((8, 2, C, N), BF16)],
        [held, quarters, pltpu.SemaphoreType.DMA((4,))],
        "y_inverse",
        None,
        [ANY],
    )
    spectral_grad, local_grad, bias_grad = run(
        outer_kernel,
        (groups,),
        [((64, 2048), BF16), ((C, C), F32), ((1, C), F32)],
        [pltpu.VMEM((1024, 128), F32)],
        "outer",
    )
    return field_grad, spectral_grad, local_grad, bias_grad.reshape(C)


def solution(mesh):
    fine = Mesh(mesh.devices.reshape(8, 8, 2, 4), GX + ("gz",))
    cells = P(GX, "gz", None, None)
    return jax.shard_map(
        local,
        mesh=fine,
        in_specs=(cells, cells, P(GX, None), P(), P()),
        out_specs=(cells, P(GX, None), P(), P()),
        check_vma=False,
    )
```

```python
import jax
import jax.numpy as jnp
import ml_dtypes
import numpy as np
from jax import lax
from jax.experimental import pallas as pl
from jax.experimental.pallas import tpu as pltpu
from jax.sharding import Mesh
from jax.sharding import PartitionSpec as P

KX = 128
KY = 64
C = 32
N = 1024
F32 = jnp.float32
BF16 = jnp.bfloat16
GX = ("y", "z", "core")
VM = pl.BlockSpec(memory_space=pltpu.VMEM)
HBM = pl.BlockSpec(memory_space=pltpu.HBM)


def angles(freq, pos):
    product = (freq[:, None].astype(np.int64) * pos[None, :].astype(np.int64)) % N
    angle = product.astype(np.float32) * np.float32(2.0 * np.pi / N)
    return np.cos(angle).astype(np.float32), np.sin(angle).astype(np.float32)


def tables():
    ycos, ysin = angles(np.arange(KY), np.arange(N))
    ytab = np.concatenate([ycos, -ysin], axis=0).astype(ml_dtypes.bfloat16)
    ytab = (ytab.astype(np.float32) / 32.0).astype(ml_dtypes.bfloat16)
    j = np.arange(KX)
    freq = np.where(j < KX // 2, j, j - KX)
    r, h, d = np.meshgrid(np.arange(4), np.arange(2), np.arange(128), indexing="ij")
    xcos, xsin = angles(freq, (8 * d + 4 * h + r).reshape(-1))
    forward = np.concatenate([xcos, xsin], axis=0).astype(ml_dtypes.bfloat16)
    inverse = forward.reshape(2 * KX, 4, 256).transpose(2, 1, 0).reshape(256, 1024)
    return ytab, forward, np.ascontiguousarray(inverse)


def nt(a, b):
    return lax.dot_general(a, b, (((1,), (1,)), ((), ())), preferred_element_type=F32)


def nn(a, b):
    return jnp.dot(a, b, preferred_element_type=F32)


def block_of(shape):
    return (lax.broadcasted_iota(jnp.int32, shape, 1) >> 5) & 3


def fold(v):
    v = v + pltpu.roll(v, 64, 1)
    return v + pltpu.roll(v, 32, 1)


def spread(base):
    block = block_of(base.shape)
    return jnp.concatenate([jnp.where(block == r, base, 0.0) for r in range(4)], axis=0).astype(BF16)


def rounded(v):
    return v.astype(BF16).astype(F32)


def mode_weight():
    first = (lax.axis_index("y") + lax.axis_index("z")) == 0
    return jnp.where(first, 1.0, 2.0).astype(F32)


def x_forward(recv, table, held, stride):
    held[...] = recv[...].astype(F32)
    parts = [
        jnp.concatenate([held[pl.ds(2 * p + h, 128, stride=stride), :] for h in range(2)], axis=0)
        for p in range(2)
    ]
    out = nn(table[...], spread(jnp.concatenate(parts, axis=1)))
    real = out[:KX, :128] + out[KX:, 128:]
    imag = out[:KX, 128:] - out[KX:, :128]
    return fold(real) * (1.0 / 32.0), fold(imag) * (1.0 / 32.0)


def paired(real, imag):
    return jnp.where((block_of(real.shape) & 1) == 0, real, imag)


def x_inverse(real, imag, table, held, stride):
    base = jnp.concatenate(
        [jnp.concatenate([real, imag], axis=1), jnp.concatenate([-imag, real], axis=1)], axis=0
    )
    out = nn(table[...], spread(base)) * (1.0 / 32.0)
    for p in range(2):
        for h in range(2):
            held[pl.ds(2 * p + h, 128, stride=stride), :] = out[
                128 * h : 128 * (h + 1), 128 * p : 128 * (p + 1)
            ]


def y_kernel(field, ytab, send, held, rows, table, sems):
    copies = [pltpu.make_async_copy(ytab, table, sems.at[4])]
    for k in range(4):
        part = field.at[pl.ds(4 * (k % 2), 4), k // 2]
        copies.append(pltpu.make_async_copy(part, rows.at[k], sems.at[k]))
    for copy in copies:
        copy.start()
    copies[0].wait()
    for k in range(4):
        z, h = k // 2, k % 2
        copies[1 + k].wait()
        out = nt(table[...], rows[k].reshape(128, N))
        for p in range(2):
            held[pl.ds(4 * z + 2 * p + h, KY, stride=8), :] = out[KY * p : KY * (p + 1)]
    send[...] = held[...].astype(BF16)


def mix_kernel(recv, weight, forward, inverse, send, kept, held):
    real, imag = x_forward(recv, forward, held, 4)
    real = rounded(real)
    imag = rounded(imag)
    kept[...] = paired(real, imag).astype(BF16)
    k = lax.broadcasted_iota(jnp.int32, (128, 1024), 0)
    lane = lax.broadcasted_iota(jnp.int32, (128, 1024), 1)
    expand = jnp.where((lane >> 5) == k, 1.0, 0.0).astype(BF16)
    wide = nn(jnp.concatenate([real, imag], axis=0).astype(BF16), expand)
    vre = jnp.zeros((KX, 128), F32)
    vim = jnp.zeros((KX, 128), F32)
    for t in range(8):
        wre = weight[:, 128 * t : 128 * (t + 1)].astype(F32)
        wim = weight[:, 1024 + 128 * t : 1024 + 128 * (t + 1)].astype(F32)
        ure = wide[:KX, 128 * t : 128 * (t + 1)]
        uim = wide[KX:, 128 * t : 128 * (t + 1)]
        vre = vre + (ure * wre - uim * wim)
        vim = vim + (ure * wim + uim * wre)
    factor = mode_weight()
    x_inverse(rounded(fold(vre) * factor), rounded(fold(vim) * factor), inverse, held, 4)
    send[...] = held[...].astype(BF16)


def point_kernel(
    recv, field, cotangent, local4, bias4, ytab, send, delta, held, wide, cots, grads, sems
):
    copies = []
    for k in range(4):
        part = cotangent.at[pl.ds(4 * (k % 2), 4), k // 2]
        copies.append(pltpu.make_async_copy(part, cots.at[k], sems.at[k]))
        copies[k].start()
    held[...] = recv[...].astype(F32)
    ones = jnp.ones((16, N), BF16)
    total = jnp.zeros((144, 128), F32)
    outs = []
    for k in range(4):
        z, h = k // 2, k % 2
        spectrum = jnp.concatenate(
            [held[pl.ds(4 * z + 2 * p + h, KY, stride=8), :] for p in range(2)], axis=0
        )
        left = jnp.concatenate([spectrum.T.astype(BF16), local4[...]], axis=1)
        rows = field[4 * h : 4 * h + 4, z].reshape(128, N)
        copies[k].wait()
        cot = cots[k].reshape(128, N)
        for part in range(4):
            cols = slice(256 * part, 256 * (part + 1))
            right = jnp.concatenate([ytab[:, cols], rows[:, cols]], axis=0)
            pre = nn(left, right) + bias4[...]
            sig = 0.5 * jnp.tanh(0.5 * pre) + 0.5
            slope = sig * (1.0 + pre * (1.0 - sig))
            grads[k, :, cols] = (cot[:, cols].astype(F32) * slope).astype(BF16)
        copies.append(pltpu.make_async_copy(grads.at[k], delta.at[k], sems.at[4 + k]))
        copies[4 + k].start()
        out = nt(jnp.concatenate([ytab[...], rows, ones], axis=0), grads[k])
        outs.append((z, h, out[:128]))
        total = total + out[128:]
    bias_total = total[128:]
    block = block_of((32, 128))
    diag = jnp.zeros((32, 128), F32)
    for r in range(4):
        diag = diag + jnp.where(block == r, total[32 * r : 32 * (r + 1)], 0.0)
    held[0:32, :] = fold(diag)
    block = block_of((8, 128))
    flat = jnp.zeros((8, 128), F32)
    for q in range(4):
        flat = flat + jnp.where(block == q, held[pl.ds(q, 8, stride=4), :], 0.0)
    bias = fold(bias_total[0:8])[0:1]
    bias_1 = rounded(bias)
    bias_2 = rounded(bias - bias_1)
    bias_3 = bias - bias_1 - bias_2
    block = block_of((1, 128))
    pieces = jnp.where(
        block == 0, bias_1, jnp.where(block == 1, bias_2, jnp.where(block == 2, bias_3, 0.0))
    )
    for z, h, out in outs:
        for p in range(2):
            wide[pl.ds(10 * z + 2 * p + h, KY, stride=20), :] = out[KY * p : KY * (p + 1)]
    for z in range(2):
        lines = [flat[4 * z + k : 4 * z + k + 1] for k in range(4)]
        lines = lines + [pieces, jnp.zeros((1, 128), F32)]
        for k, line in enumerate(lines):
            wide[pl.ds(10 * z + 4 + k, KY, stride=20), :] = jnp.broadcast_to(line, (KY, 128))
    send[...] = wide[...].astype(BF16)
    for copy in copies[4:]:
        copy.wait()


def back_kernel(recv, forward, kept, share, held):
    real, imag = x_forward(recv, forward, held, 10)
    factor = mode_weight()
    real = rounded(real * factor)
    imag = rounded(imag * factor)
    kept[:KX] = real
    kept[KX:] = imag
    share[:KX] = paired(real, imag).astype(BF16)
    lines = [
        jnp.sum(held[pl.ds(4 + k, 128, stride=10), :], axis=0, keepdims=True) for k in range(5)
    ]
    total = jnp.concatenate(lines[:4], axis=0)
    bias = fold(lines[4])
    share[KX:] = jnp.concatenate(
        [
            rounded(total),
            total - rounded(total),
            rounded(bias),
            bias - rounded(bias),
            jnp.zeros((6, 128), F32),
        ],
        axis=0,
    ).astype(BF16)


def adjoint_kernel(kept, weight, inverse, firsts, seconds, send, group, held, high, low):
    dre = kept[:KX]
    dim = kept[KX:]
    for t in range(8):
        cols = slice(128 * t, 128 * (t + 1))
        wre = weight[:, cols].astype(F32)
        wim = weight[:, 1024 + 128 * t : 1024 + 128 * (t + 1)].astype(F32)
        for k, term in ((0, dre * wre + dim * wim), (1, dim * wre - dre * wim)):
            top = term.astype(BF16)
            high[KX * k : KX * (k + 1), cols] = top
            low[KX * k : KX * (k + 1), cols] = (term - top.astype(F32)).astype(BF16)
    k = lax.broadcasted_iota(jnp.int32, (1024, 128), 0)
    lane = lax.broadcasted_iota(jnp.int32, (1024, 128), 1)
    gather = jnp.where((k >> 5) == (lane & 31), 1.0, 0.0).astype(BF16)
    back = rounded(nn(high[...], gather) + nn(low[...], gather))
    x_inverse(back[:KX], back[KX:], inverse, held, 4)
    send[...] = held[...].astype(BF16)
    start = 64 * lax.axis_index("core")
    left = block_of((64, 128)) < 2
    for k, (both, step) in enumerate(((firsts, KX), (seconds, KX + 16))):
        one = both[pl.ds(pl.multiple_of(start, 16), 64), :].astype(F32)
        two = both[pl.ds(pl.multiple_of(step + start, 16), 64), :].astype(F32)
        group[64 * k : 64 * (k + 1)] = jnp.where(left, one, two).astype(BF16)
    group[128:144] = seconds[KX : KX + 16]
    group[144:160] = seconds[2 * KX + 16 : 2 * KX + 32]


def grad_kernel(recv, delta, local4, ytab, field_grad, held, rows, sems):
    held[...] = recv[...].astype(F32)
    copies = []
    for k in range(4):
        z, h = k // 2, k % 2
        spectrum = jnp.concatenate(
            [held[pl.ds(4 * z + 2 * p + h, KY, stride=8), :] for p in range(2)], axis=0
        )
        left = jnp.concatenate([spectrum.T.astype(BF16), local4[...]], axis=1)
        for part in range(4):
            cols = slice(256 * part, 256 * (part + 1))
            right = jnp.concatenate([ytab[:, cols], delta[k, :, cols]], axis=0)
            rows[k, :, :, cols] = nn(left, right).astype(BF16).reshape(4, 32, 256)
        copies.append(
            pltpu.make_async_copy(rows.at[k], field_grad.at[pl.ds(4 * h, 4), z], sems.at[k])
        )
        copies[k].start()
    for copy in copies:
        copy.wait()


def outer_kernel(groups, out, local_grad, bias_grad, tiles):
    lane = lax.broadcasted_iota(jnp.int32, (128, 1024), 1)
    k = lax.broadcasted_iota(jnp.int32, (128, 1024), 0)
    expand = jnp.where((lane >> 5) == k, 1.0, 0.0).astype(BF16)
    first = jnp.concatenate([groups[160 * g : 160 * g + 64] for g in range(4)], axis=0).astype(F32)
    turned = [first] + [pltpu.roll(first, 128 - 32 * b, 1) for b in range(1, 4)]
    compact = jnp.concatenate(turned, axis=0).astype(BF16)
    block = block_of((64, 128))
    for g in range(4):
        second = groups[160 * g + 64 : 160 * g + 128].astype(F32)
        for b in range(4):
            tiles[64 * (4 * g + b) : 64 * (4 * g + b + 1)] = fold(
                jnp.where(block == b, second, 0.0)
            )
    for pair in range(4):
        wide = nn(compact, expand[:, 256 * pair : 256 * (pair + 1)])
        for half in range(2):
            t = 2 * pair + half
            cols = slice(128 * half, 128 * (half + 1))
            real = jnp.zeros((64, 128), F32)
            imag = jnp.zeros((64, 128), F32)
            for g in range(4):
                for z in range(2):
                    b = 2 * z
                    ure = wide[256 * b + 64 * g : 256 * b + 64 * (g + 1), cols]
                    uim = wide[256 * (b + 1) + 64 * g : 256 * (b + 1) + 64 * (g + 1), cols]
                    dre = tiles[64 * (4 * g + b) : 64 * (4 * g + b + 1)]
                    dim = tiles[64 * (4 * g + b + 1) : 64 * (4 * g + b + 2)]
                    real = real + (ure * dre + uim * dim)
                    imag = imag + (ure * dim - uim * dre)
            out[:, 128 * t : 128 * (t + 1)] = real.astype(BF16)
            out[:, 1024 + 128 * t : 1024 + 128 * (t + 1)] = imag.astype(BF16)
    gscale = float((N * N * 8) ** -0.5)
    total = groups[128:160].astype(F32)
    for g in range(1, 4):
        total = total + groups[160 * g + 128 : 160 * g + 160].astype(F32)
    flat = jnp.concatenate(
        [total[0:4] + total[4:8], total[16:20] + total[20:24]], axis=0
    ) * gscale
    for q in range(4):
        local_grad[pl.ds(q, 8, stride=4), :] = flat[:, 32 * q : 32 * (q + 1)]
    bias_grad[...] = ((total[8:9] + total[9:10]) * gscale)[:, :32]


def run(kernel, operands, outs, scratch, name, specs=None, out_specs=None):
    shapes = [jax.ShapeDtypeStruct(shape, dtype) for shape, dtype in outs]
    return pl.pallas_call(
        kernel,
        out_shape=shapes,
        in_specs=specs or [VM] * len(operands),
        out_specs=out_specs or [VM] * len(shapes),
        scratch_shapes=scratch,
        compiler_params=pltpu.CompilerParams(vmem_limit_bytes=16 * 1024 * 1024),
        cost_estimate=pl.CostEstimate(
            flops=200_000_000, bytes_accessed=1 << 20, transcendentals=0
        ),
        name=name,
    )(*operands)


def exchange(values, *shape):
    blocks = values.reshape((128,) + shape)
    return lax.all_to_all(blocks, GX, 0, 0, tiled=True).reshape(values.shape)


def local(field, cotangent, spectral_weight, local_weight, bias):
    ytab, forward, inverse = (jnp.asarray(table) for table in tables())
    same = jnp.asarray(np.kron(np.eye(4), np.ones((C, C))).astype(ml_dtypes.bfloat16))
    local_in = jnp.tile(local_weight, (4, 4)) * same
    local_out = jnp.tile(local_weight.T, (4, 4)) * same
    bias4 = jnp.tile(bias, 4)[:, None]
    slab = ((512, 128), BF16)
    slab_wide = ((1280, 128), BF16)
    held = pltpu.VMEM((512, 128), F32)
    held_wide = pltpu.VMEM((1280, 128), F32)
    quarters = pltpu.VMEM((4, 4, C, N), BF16)

    (send,) = run(
        y_kernel,
        (field, ytab),
        [slab],
        [held, quarters, pltpu.VMEM((128, N), BF16), pltpu.SemaphoreType.DMA((5,))],
        "y_forward",
        [HBM, HBM],
    )
    recv = exchange(send, 4, 128)
    weight = lax.all_gather(spectral_weight, "core", axis=0, tiled=True)
    send, first = run(
        mix_kernel,
        (recv, weight, forward, inverse),
        [slab, ((KX, 128), BF16)],
        [held],
        "mix",
    )
    recv = exchange(send, 4, 128)
    firsts = lax.all_gather(first, "core", axis=0, tiled=True)
    send, delta = run(
        point_kernel,
        (recv, field, cotangent, local_out, bias4, ytab),
        [slab_wide, ((4, 128, N), BF16)],
        [
            held,
            held_wide,
            quarters,
            pltpu.VMEM((4, 128, N), BF16),
            pltpu.SemaphoreType.DMA((8,)),
        ],
        "pointwise",
        [VM, VM, HBM, VM, VM, VM],
        [VM, HBM],
    )
    recv = exchange(send, 5, 2, 128)
    second, share = run(
        back_kernel,
        (recv, forward),
        [((2 * KX, 128), F32), ((KX + 16, 128), BF16)],
        [held_wide],
        "x_forward",
    )
    seconds = lax.all_gather(share, "core", axis=0, tiled=True)
    send, group = run(
        adjoint_kernel,
        (second, weight, inverse, firsts, seconds),
        [slab, ((160, 128), BF16)],
        [held, pltpu.VMEM((256, 1024), BF16), pltpu.VMEM((256, 1024), BF16)],
        "adjoint",
    )
    recv = exchange(send, 4, 128)
    groups = lax.all_gather(group, "gz", axis=0, tiled=True)
    (field_grad,) = run(
        grad_kernel,
        (recv, delta, local_in, ytab),
        [((8, 2, C, N), BF16)],
        [held, quarters, pltpu.SemaphoreType.DMA((4,))],
        "y_inverse",
        None,
        [HBM],
    )
    spectral_grad, local_grad, bias_grad = run(
        outer_kernel,
        (groups,),
        [((64, 2048), BF16), ((C, C), F32), ((1, C), F32)],
        [pltpu.VMEM((1024, 128), F32)],
        "outer",
    )
    return field_grad, spectral_grad, local_grad, bias_grad.reshape(C)


def solution(mesh):
    fine = Mesh(mesh.devices.reshape(8, 8, 2, 4), GX + ("gz",))
    cells = P(GX, "gz", None, None)
    return jax.shard_map(
        local,
        mesh=fine,
        in_specs=(cells, cells, P(GX, None), P(), P()),
        out_specs=(cells, P(GX, None), P(), P()),
        check_vma=False,
    )
```

```python
import jax
import jax.numpy as jnp
import ml_dtypes
import numpy as np
from jax import lax
from jax.experimental import pallas as pl
from jax.experimental.pallas import tpu as pltpu
from jax.sharding import Mesh
from jax.sharding import PartitionSpec as P

KX = 128
KY = 64
C = 32
N = 1024
F32 = jnp.float32
BF16 = jnp.bfloat16
GX = ("y", "z", "core")
VM = pl.BlockSpec(memory_space=pltpu.VMEM)
HBM = pl.BlockSpec(memory_space=pltpu.HBM)


def angles(freq, pos):
    product = (freq[:, None].astype(np.int64) * pos[None, :].astype(np.int64)) % N
    angle = product.astype(np.float32) * np.float32(2.0 * np.pi / N)
    return np.cos(angle).astype(np.float32), np.sin(angle).astype(np.float32)


def tables():
    ycos, ysin = angles(np.arange(KY), np.arange(N))
    ytab = np.concatenate([ycos, -ysin], axis=0).astype(ml_dtypes.bfloat16)
    ytab = (ytab.astype(np.float32) / 32.0).astype(ml_dtypes.bfloat16)
    j = np.arange(KX)
    freq = np.where(j < KX // 2, j, j - KX)
    r, h, d = np.meshgrid(np.arange(4), np.arange(2), np.arange(128), indexing="ij")
    xcos, xsin = angles(freq, (8 * d + 4 * h + r).reshape(-1))
    forward = np.concatenate([xcos, xsin], axis=0).astype(ml_dtypes.bfloat16)
    inverse = forward.reshape(2 * KX, 4, 256).transpose(2, 1, 0).reshape(256, 1024)
    return ytab, forward, np.ascontiguousarray(inverse)


def nt(a, b):
    return lax.dot_general(a, b, (((1,), (1,)), ((), ())), preferred_element_type=F32)


def nn(a, b):
    return jnp.dot(a, b, preferred_element_type=F32)


def block_of(shape):
    return (lax.broadcasted_iota(jnp.int32, shape, 1) >> 5) & 3


def fold(v):
    v = v + pltpu.roll(v, 64, 1)
    return v + pltpu.roll(v, 32, 1)


def spread(base):
    block = block_of(base.shape)
    return jnp.concatenate([jnp.where(block == r, base, 0.0) for r in range(4)], axis=0).astype(BF16)


def rounded(v):
    return v.astype(BF16).astype(F32)


def mode_weight():
    first = (lax.axis_index("y") + lax.axis_index("z")) == 0
    return jnp.where(first, 1.0, 2.0).astype(F32)


def x_forward(recv, table, held, stride):
    held[...] = recv[...].astype(F32)
    parts = [
        jnp.concatenate([held[pl.ds(2 * p + h, 128, stride=stride), :] for h in range(2)], axis=0)
        for p in range(2)
    ]
    out = nn(table[...], spread(jnp.concatenate(parts, axis=1)))
    real = out[:KX, :128] + out[KX:, 128:]
    imag = out[:KX, 128:] - out[KX:, :128]
    return fold(real) * (1.0 / 32.0), fold(imag) * (1.0 / 32.0)


def paired(real, imag):
    return jnp.where((block_of(real.shape) & 1) == 0, real, imag)


def x_inverse(real, imag, table, held, stride):
    base = jnp.concatenate(
        [jnp.concatenate([real, imag], axis=1), jnp.concatenate([-imag, real], axis=1)], axis=0
    )
    out = nn(table[...], spread(base)) * (1.0 / 32.0)
    for p in range(2):
        for h in range(2):
            held[pl.ds(2 * p + h, 128, stride=stride), :] = out[
                128 * h : 128 * (h + 1), 128 * p : 128 * (p + 1)
            ]


def y_kernel(field, ytab, send, held, rows, table, sems):
    copies = [pltpu.make_async_copy(ytab, table, sems.at[4])]
    for k in range(4):
        part = field.at[pl.ds(4 * (k % 2), 4), k // 2]
        copies.append(pltpu.make_async_copy(part, rows.at[k], sems.at[k]))
    for copy in copies:
        copy.start()
    copies[0].wait()
    for k in range(4):
        z, h = k // 2, k % 2
        copies[1 + k].wait()
        out = nt(table[...], rows[k].reshape(128, N))
        for p in range(2):
            held[pl.ds(4 * z + 2 * p + h, KY, stride=8), :] = out[KY * p : KY * (p + 1)]
    send[...] = held[...].astype(BF16)


def mix_kernel(recv, weight, forward, inverse, send, kept, held):
    real, imag = x_forward(recv, forward, held, 4)
    real = rounded(real)
    imag = rounded(imag)
    kept[...] = paired(real, imag).astype(BF16)
    k = lax.broadcasted_iota(jnp.int32, (128, 1024), 0)
    lane = lax.broadcasted_iota(jnp.int32, (128, 1024), 1)
    expand = jnp.where((lane >> 5) == k, 1.0, 0.0).astype(BF16)
    wide = nn(jnp.concatenate([real, imag], axis=0).astype(BF16), expand)
    vre = jnp.zeros((KX, 128), F32)
    vim = jnp.zeros((KX, 128), F32)
    for t in range(8):
        wre = weight[:, 128 * t : 128 * (t + 1)].astype(F32)
        wim = weight[:, 1024 + 128 * t : 1024 + 128 * (t + 1)].astype(F32)
        ure = wide[:KX, 128 * t : 128 * (t + 1)]
        uim = wide[KX:, 128 * t : 128 * (t + 1)]
        vre = vre + (ure * wre - uim * wim)
        vim = vim + (ure * wim + uim * wre)
    factor = mode_weight()
    x_inverse(rounded(fold(vre) * factor), rounded(fold(vim) * factor), inverse, held, 4)
    send[...] = held[...].astype(BF16)


def point_kernel(
    recv, field, cotangent, local4, bias4, ytab, send, delta, held, wide, cots, grads, sems
):
    copies = []
    for k in range(4):
        part = cotangent.at[pl.ds(4 * (k % 2), 4), k // 2]
        copies.append(pltpu.make_async_copy(part, cots.at[k], sems.at[k]))
        copies[k].start()
    held[...] = recv[...].astype(F32)
    ones = jnp.ones((16, N), BF16)
    total = jnp.zeros((144, 128), F32)
    outs = []
    for k in range(4):
        z, h = k // 2, k % 2
        spectrum = jnp.concatenate(
            [held[pl.ds(4 * z + 2 * p + h, KY, stride=8), :] for p in range(2)], axis=0
        )
        left = jnp.concatenate([spectrum.T.astype(BF16), local4[...]], axis=1)
        rows = field[4 * h : 4 * h + 4, z].reshape(128, N)
        copies[k].wait()
        cot = cots[k].reshape(128, N)
        for part in range(4):
            cols = slice(256 * part, 256 * (part + 1))
            right = jnp.concatenate([ytab[:, cols], rows[:, cols]], axis=0)
            pre = nn(left, right) + bias4[...]
            sig = 0.5 * jnp.tanh(0.5 * pre) + 0.5
            slope = sig * (1.0 + pre * (1.0 - sig))
            grads[k, :, cols] = (cot[:, cols].astype(F32) * slope).astype(BF16)
        copies.append(pltpu.make_async_copy(grads.at[k], delta.at[k], sems.at[4 + k]))
        copies[4 + k].start()
        out = nt(jnp.concatenate([ytab[...], rows, ones], axis=0), grads[k])
        outs.append((z, h, out[:128]))
        total = total + out[128:]
    bias_total = total[128:]
    block = block_of((32, 128))
    diag = jnp.zeros((32, 128), F32)
    for r in range(4):
        diag = diag + jnp.where(block == r, total[32 * r : 32 * (r + 1)], 0.0)
    held[0:32, :] = fold(diag)
    block = block_of((8, 128))
    flat = jnp.zeros((8, 128), F32)
    for q in range(4):
        flat = flat + jnp.where(block == q, held[pl.ds(q, 8, stride=4), :], 0.0)
    bias = fold(bias_total[0:8])[0:1]
    bias_1 = rounded(bias)
    bias_2 = rounded(bias - bias_1)
    bias_3 = bias - bias_1 - bias_2
    block = block_of((1, 128))
    pieces = jnp.where(
        block == 0, bias_1, jnp.where(block == 1, bias_2, jnp.where(block == 2, bias_3, 0.0))
    )
    for z, h, out in outs:
        for p in range(2):
            wide[pl.ds(10 * z + 2 * p + h, KY, stride=20), :] = out[KY * p : KY * (p + 1)]
    for z in range(2):
        lines = [flat[4 * z + k : 4 * z + k + 1] for k in range(4)]
        lines = lines + [pieces, jnp.zeros((1, 128), F32)]
        for k, line in enumerate(lines):
            wide[pl.ds(10 * z + 4 + k, KY, stride=20), :] = jnp.broadcast_to(line, (KY, 128))
    send[...] = wide[...].astype(BF16)
    for copy in copies[4:]:
        copy.wait()


def back_kernel(recv, forward, kept, share, held):
    real, imag = x_forward(recv, forward, held, 10)
    factor = mode_weight()
    real = rounded(real * factor)
    imag = rounded(imag * factor)
    kept[:KX] = real
    kept[KX:] = imag
    share[:KX] = paired(real, imag).astype(BF16)
    lines = [
        jnp.sum(held[pl.ds(4 + k, 128, stride=10), :], axis=0, keepdims=True) for k in range(5)
    ]
    total = jnp.concatenate(lines[:4], axis=0)
    bias = fold(lines[4])
    share[KX:] = jnp.concatenate(
        [
            rounded(total),
            total - rounded(total),
            rounded(bias),
            bias - rounded(bias),
            jnp.zeros((6, 128), F32),
        ],
        axis=0,
    ).astype(BF16)


def adjoint_kernel(kept, weight, inverse, firsts, seconds, send, group, held, high, low):
    dre = kept[:KX]
    dim = kept[KX:]
    for t in range(8):
        cols = slice(128 * t, 128 * (t + 1))
        wre = weight[:, cols].astype(F32)
        wim = weight[:, 1024 + 128 * t : 1024 + 128 * (t + 1)].astype(F32)
        for k, term in ((0, dre * wre + dim * wim), (1, dim * wre - dre * wim)):
            top = term.astype(BF16)
            high[KX * k : KX * (k + 1), cols] = top
            low[KX * k : KX * (k + 1), cols] = (term - top.astype(F32)).astype(BF16)
    k = lax.broadcasted_iota(jnp.int32, (1024, 128), 0)
    lane = lax.broadcasted_iota(jnp.int32, (1024, 128), 1)
    gather = jnp.where((k >> 5) == (lane & 31), 1.0, 0.0).astype(BF16)
    back = rounded(nn(high[...], gather) + nn(low[...], gather))
    x_inverse(back[:KX], back[KX:], inverse, held, 4)
    send[...] = held[...].astype(BF16)
    start = 64 * lax.axis_index("core")
    left = block_of((64, 128)) < 2
    for k, (both, step) in enumerate(((firsts, KX), (seconds, KX + 16))):
        one = both[pl.ds(pl.multiple_of(start, 16), 64), :].astype(F32)
        two = both[pl.ds(pl.multiple_of(step + start, 16), 64), :].astype(F32)
        group[64 * k : 64 * (k + 1)] = jnp.where(left, one, two).astype(BF16)
    group[128:144] = seconds[KX : KX + 16]
    group[144:160] = seconds[2 * KX + 16 : 2 * KX + 32]


def grad_kernel(recv, delta, local4, ytab, field_grad, held, rows, sems):
    held[...] = recv[...].astype(F32)
    copies = []
    for k in range(4):
        z, h = k // 2, k % 2
        spectrum = jnp.concatenate(
            [held[pl.ds(4 * z + 2 * p + h, KY, stride=8), :] for p in range(2)], axis=0
        )
        left = jnp.concatenate([spectrum.T.astype(BF16), local4[...]], axis=1)
        for part in range(4):
            cols = slice(256 * part, 256 * (part + 1))
            right = jnp.concatenate([ytab[:, cols], delta[k, :, cols]], axis=0)
            rows[k, :, :, cols] = nn(left, right).astype(BF16).reshape(4, 32, 256)
        copies.append(
            pltpu.make_async_copy(rows.at[k], field_grad.at[pl.ds(4 * h, 4), z], sems.at[k])
        )
        copies[k].start()
    for copy in copies:
        copy.wait()


def outer_kernel(groups, out, local_grad, bias_grad, tiles):
    lane = lax.broadcasted_iota(jnp.int32, (128, 1024), 1)
    k = lax.broadcasted_iota(jnp.int32, (128, 1024), 0)
    expand = jnp.where((lane >> 5) == k, 1.0, 0.0).astype(BF16)
    first = jnp.concatenate([groups[160 * g : 160 * g + 64] for g in range(4)], axis=0).astype(F32)
    turned = [first] + [pltpu.roll(first, 128 - 32 * b, 1) for b in range(1, 4)]
    compact = jnp.concatenate(turned, axis=0).astype(BF16)
    block = block_of((64, 128))
    for g in range(4):
        second = groups[160 * g + 64 : 160 * g + 128].astype(F32)
        for b in range(4):
            tiles[64 * (4 * g + b) : 64 * (4 * g + b + 1)] = fold(
                jnp.where(block == b, second, 0.0)
            )
    for pair in range(4):
        wide = nn(compact, expand[:, 256 * pair : 256 * (pair + 1)])
        for half in range(2):
            t = 2 * pair + half
            cols = slice(128 * half, 128 * (half + 1))
            real = jnp.zeros((64, 128), F32)
            imag = jnp.zeros((64, 128), F32)
            for g in range(4):
                for z in range(2):
                    b = 2 * z
                    ure = wide[256 * b + 64 * g : 256 * b + 64 * (g + 1), cols]
                    uim = wide[256 * (b + 1) + 64 * g : 256 * (b + 1) + 64 * (g + 1), cols]
                    dre = tiles[64 * (4 * g + b) : 64 * (4 * g + b + 1)]
                    dim = tiles[64 * (4 * g + b + 1) : 64 * (4 * g + b + 2)]
                    real = real + (ure * dre + uim * dim)
                    imag = imag + (ure * dim - uim * dre)
            out[:, 128 * t : 128 * (t + 1)] = real.astype(BF16)
            out[:, 1024 + 128 * t : 1024 + 128 * (t + 1)] = imag.astype(BF16)
    gscale = float((N * N * 8) ** -0.5)
    total = groups[128:160].astype(F32)
    for g in range(1, 4):
        total = total + groups[160 * g + 128 : 160 * g + 160].astype(F32)
    flat = jnp.concatenate(
        [total[0:4] + total[4:8], total[16:20] + total[20:24]], axis=0
    ) * gscale
    for q in range(4):
        local_grad[pl.ds(q, 8, stride=4), :] = flat[:, 32 * q : 32 * (q + 1)]
    bias_grad[...] = ((total[8:9] + total[9:10]) * gscale)[:, :32]


def run(kernel, operands, outs, scratch, name, specs=None, out_specs=None):
    specs = specs or [VM] * len(operands)
    out_specs = out_specs or [VM] * len(outs)
    operands = [
        pltpu.with_memory_space_constraint(operand, pltpu.HBM) if spec is HBM else operand
        for operand, spec in zip(operands, specs)
    ]
    return pl.pallas_call(
        kernel,
        out_shape=[
            (pltpu.HBM if spec is HBM else jax.ShapeDtypeStruct)(*out)
            for out, spec in zip(outs, out_specs)
        ],
        in_specs=specs,
        out_specs=out_specs,
        scratch_shapes=scratch,
        compiler_params=pltpu.CompilerParams(vmem_limit_bytes=16 * 1024 * 1024),
        cost_estimate=pl.CostEstimate(
            flops=200_000_000, bytes_accessed=1 << 20, transcendentals=0
        ),
        name=name,
    )(*operands)


def exchange(values, *shape):
    blocks = values.reshape((128,) + shape)
    return lax.all_to_all(blocks, GX, 0, 0, tiled=True).reshape(values.shape)


def local(field, cotangent, spectral_weight, local_weight, bias):
    ytab, forward, inverse = (jnp.asarray(table) for table in tables())
    same = jnp.asarray(np.kron(np.eye(4), np.ones((C, C))).astype(ml_dtypes.bfloat16))
    local_in = jnp.tile(local_weight, (4, 4)) * same
    local_out = jnp.tile(local_weight.T, (4, 4)) * same
    bias4 = jnp.tile(bias, 4)[:, None]
    slab = ((512, 128), BF16)
    slab_wide = ((1280, 128), BF16)
    held = pltpu.VMEM((512, 128), F32)
    held_wide = pltpu.VMEM((1280, 128), F32)
    quarters = pltpu.VMEM((4, 4, C, N), BF16)

    (send,) = run(
        y_kernel,
        (field, ytab),
        [slab],
        [held, quarters, pltpu.VMEM((128, N), BF16), pltpu.SemaphoreType.DMA((5,))],
        "y_forward",
        [HBM, HBM],
    )
    recv = exchange(send, 4, 128)
    weight = lax.all_gather(spectral_weight, "core", axis=0, tiled=True)
    send, first = run(
        mix_kernel,
        (recv, weight, forward, inverse),
        [slab, ((KX, 128), BF16)],
        [held],
        "mix",
    )
    recv = exchange(send, 4, 128)
    firsts = lax.all_gather(first, "core", axis=0, tiled=True)
    send, delta = run(
        point_kernel,
        (recv, field, cotangent, local_out, bias4, ytab),
        [slab_wide, ((4, 128, N), BF16)],
        [
            held,
            held_wide,
            quarters,
            pltpu.VMEM((4, 128, N), BF16),
            pltpu.SemaphoreType.DMA((8,)),
        ],
        "pointwise",
        [VM, VM, HBM, VM, VM, VM],
        [VM, HBM],
    )
    recv = exchange(send, 5, 2, 128)
    second, share = run(
        back_kernel,
        (recv, forward),
        [((2 * KX, 128), F32), ((KX + 16, 128), BF16)],
        [held_wide],
        "x_forward",
    )
    seconds = lax.all_gather(share, "core", axis=0, tiled=True)
    send, group = run(
        adjoint_kernel,
        (second, weight, inverse, firsts, seconds),
        [slab, ((160, 128), BF16)],
        [held, pltpu.VMEM((256, 1024), BF16), pltpu.VMEM((256, 1024), BF16)],
        "adjoint",
    )
    recv = exchange(send, 4, 128)
    groups = lax.all_gather(group, "gz", axis=0, tiled=True)
    (field_grad,) = run(
        grad_kernel,
        (recv, delta, local_in, ytab),
        [((8, 2, C, N), BF16)],
        [held, quarters, pltpu.SemaphoreType.DMA((4,))],
        "y_inverse",
        None,
        [HBM],
    )
    spectral_grad, local_grad, bias_grad = run(
        outer_kernel,
        (groups,),
        [((64, 2048), BF16), ((C, C), F32), ((1, C), F32)],
        [pltpu.VMEM((1024, 128), F32)],
        "outer",
    )
    return field_grad, spectral_grad, local_grad, bias_grad.reshape(C)


def solution(mesh):
    fine = Mesh(mesh.devices.reshape(8, 8, 2, 4), GX + ("gz",))
    cells = P(GX, "gz", None, None)
    return jax.shard_map(
        local,
        mesh=fine,
        in_specs=(cells, cells, P(GX, None), P(), P()),
        out_specs=(cells, P(GX, None), P(), P()),
        check_vma=False,
    )
```

```python
import jax
import jax.numpy as jnp
import ml_dtypes
import numpy as np
from jax import lax
from jax.experimental import pallas as pl
from jax.experimental.pallas import tpu as pltpu
from jax.sharding import Mesh
from jax.sharding import PartitionSpec as P

KX = 128
KY = 64
C = 32
N = 1024
F32 = jnp.float32
BF16 = jnp.bfloat16
GX = ("y", "z", "core")
VM = pl.BlockSpec(memory_space=pltpu.VMEM)
HBM = pl.BlockSpec(memory_space=pltpu.HBM)


def angles(freq, pos):
    product = (freq[:, None].astype(np.int64) * pos[None, :].astype(np.int64)) % N
    angle = product.astype(np.float32) * np.float32(2.0 * np.pi / N)
    return np.cos(angle).astype(np.float32), np.sin(angle).astype(np.float32)


def tables():
    ycos, ysin = angles(np.arange(KY), np.arange(N))
    ytab = np.concatenate([ycos, -ysin], axis=0).astype(ml_dtypes.bfloat16)
    ytab = (ytab.astype(np.float32) / 32.0).astype(ml_dtypes.bfloat16)
    j = np.arange(KX)
    freq = np.where(j < KX // 2, j, j - KX)
    r, h, d = np.meshgrid(np.arange(4), np.arange(2), np.arange(128), indexing="ij")
    xcos, xsin = angles(freq, (8 * d + 4 * h + r).reshape(-1))
    forward = np.concatenate([xcos, xsin], axis=0).astype(ml_dtypes.bfloat16)
    inverse = forward.reshape(2 * KX, 4, 256).transpose(2, 1, 0).reshape(256, 1024)
    return ytab, forward, np.ascontiguousarray(inverse)


def nt(a, b):
    return lax.dot_general(a, b, (((1,), (1,)), ((), ())), preferred_element_type=F32)


def nn(a, b):
    return jnp.dot(a, b, preferred_element_type=F32)


def block_of(shape):
    return (lax.broadcasted_iota(jnp.int32, shape, 1) >> 5) & 3


def fold(v):
    v = v + pltpu.roll(v, 64, 1)
    return v + pltpu.roll(v, 32, 1)


def spread(base):
    block = block_of(base.shape)
    return jnp.concatenate([jnp.where(block == r, base, 0.0) for r in range(4)], axis=0).astype(BF16)


def rounded(v):
    return v.astype(BF16).astype(F32)


def mode_weight():
    first = (lax.axis_index("y") + lax.axis_index("z")) == 0
    return jnp.where(first, 1.0, 2.0).astype(F32)


def x_forward(recv, table, held, stride):
    held[...] = recv[...].astype(F32)
    parts = [
        jnp.concatenate([held[pl.ds(2 * p + h, 128, stride=stride), :] for h in range(2)], axis=0)
        for p in range(2)
    ]
    out = nn(table[...], spread(jnp.concatenate(parts, axis=1)))
    real = out[:KX, :128] + out[KX:, 128:]
    imag = out[:KX, 128:] - out[KX:, :128]
    return fold(real) * (1.0 / 32.0), fold(imag) * (1.0 / 32.0)


def paired(real, imag):
    return jnp.where((block_of(real.shape) & 1) == 0, real, imag)


def x_inverse(real, imag, table, held, stride):
    base = jnp.concatenate(
        [jnp.concatenate([real, imag], axis=1), jnp.concatenate([-imag, real], axis=1)], axis=0
    )
    out = nn(table[...], spread(base)) * (1.0 / 32.0)
    for p in range(2):
        for h in range(2):
            held[pl.ds(2 * p + h, 128, stride=stride), :] = out[
                128 * h : 128 * (h + 1), 128 * p : 128 * (p + 1)
            ]


def y_kernel(field, ytab, send, held, rows, table, sems):
    copies = [pltpu.make_async_copy(ytab, table, sems.at[4])]
    for k in range(4):
        part = field.at[pl.ds(4 * (k % 2), 4), k // 2]
        copies.append(pltpu.make_async_copy(part, rows.at[k], sems.at[k]))
    for copy in copies:
        copy.start()
    for k in range(4):
        z, h = k // 2, k % 2
        if h == 0:
            for copy in copies[3 * z : 3 + 2 * z]:
                copy.wait()
        out = nt(table[...], rows[k].reshape(128, N))
        for p in range(2):
            held[pl.ds(4 * z + 2 * p + h, KY, stride=8), :] = out[KY * p : KY * (p + 1)]
    send[...] = held[...].astype(BF16)


def mix_kernel(recv, weight, forward, inverse, send, kept, held):
    real, imag = x_forward(recv, forward, held, 4)
    real = rounded(real)
    imag = rounded(imag)
    kept[...] = paired(real, imag).astype(BF16)
    k = lax.broadcasted_iota(jnp.int32, (128, 1024), 0)
    lane = lax.broadcasted_iota(jnp.int32, (128, 1024), 1)
    expand = jnp.where((lane >> 5) == k, 1.0, 0.0).astype(BF16)
    wide = nn(jnp.concatenate([real, imag], axis=0).astype(BF16), expand)
    vre = jnp.zeros((KX, 128), F32)
    vim = jnp.zeros((KX, 128), F32)
    for t in range(8):
        wre = weight[:, 128 * t : 128 * (t + 1)].astype(F32)
        wim = weight[:, 1024 + 128 * t : 1024 + 128 * (t + 1)].astype(F32)
        ure = wide[:KX, 128 * t : 128 * (t + 1)]
        uim = wide[KX:, 128 * t : 128 * (t + 1)]
        vre = vre + (ure * wre - uim * wim)
        vim = vim + (ure * wim + uim * wre)
    factor = mode_weight()
    x_inverse(rounded(fold(vre) * factor), rounded(fold(vim) * factor), inverse, held, 4)
    send[...] = held[...].astype(BF16)


def point_kernel(
    recv, field, cotangent, local, bias, ytab, send, delta, held, wide, cot, grad, early, sems
):
    copies = [
        pltpu.make_async_copy(cotangent, cot, sems.at[0]),
        pltpu.make_async_copy(grad, delta, sems.at[1]),
    ]
    copies[0].start()
    held[...] = recv[...].astype(F32)
    row = lax.broadcasted_iota(jnp.int32, (128, C), 0)
    same = jnp.where((row & 31) == lax.broadcasted_iota(jnp.int32, (128, C), 1), 1.0, 0.0)
    bias4 = jnp.sum(same * bias[...], axis=1, keepdims=True)
    same = same.astype(BF16)
    local4 = nt(nt(same, local[...]).astype(BF16), same)
    row = lax.broadcasted_iota(jnp.int32, (128, 128), 0)
    local4 = jnp.where((row >> 5) == block_of((128, 128)), local4, 0.0).astype(BF16)

    def rows_of(ref, k):
        return ref[4 * (k % 2) : 4 * (k % 2) + 4, k // 2].reshape(128, N)

    lefts = []
    for k in range(4):
        spectrum = jnp.concatenate(
            [held[pl.ds(4 * (k // 2) + 2 * p + k % 2, KY, stride=8), :] for p in range(2)], axis=0
        )
        lefts.append(jnp.concatenate([spectrum.T.astype(BF16), local4], axis=1))

    def before(k, cols):
        right = jnp.concatenate([ytab[:, cols], rows_of(field, k)[:, cols]], axis=0)
        return nn(lefts[k], right) + bias4

    parts = [slice(256 * part, 256 * (part + 1)) for part in range(4)]
    for cols in parts:
        early[:, cols] = before(0, cols)
    copies[0].wait()
    for k in range(4):
        for cols in parts:
            pre = early[:, cols] if k == 0 else before(k, cols)
            sig = 0.5 * jnp.tanh(0.5 * pre) + 0.5
            slope = sig * (1.0 + pre * (1.0 - sig))
            grad[k, :, cols] = (rows_of(cot, k)[:, cols].astype(F32) * slope).astype(BF16)
    copies[1].start()
    ones = jnp.ones((16, N), BF16)
    total = jnp.zeros((144, 128), F32)
    outs = []
    for k in range(4):
        out = nt(jnp.concatenate([ytab[...], rows_of(field, k), ones], axis=0), grad[k])
        outs.append((k // 2, k % 2, out[:128]))
        total = total + out[128:]
    bias_total = total[128:]
    block = block_of((32, 128))
    diag = jnp.zeros((32, 128), F32)
    for r in range(4):
        diag = diag + jnp.where(block == r, total[32 * r : 32 * (r + 1)], 0.0)
    held[0:32, :] = fold(diag)
    block = block_of((8, 128))
    flat = jnp.zeros((8, 128), F32)
    for q in range(4):
        flat = flat + jnp.where(block == q, held[pl.ds(q, 8, stride=4), :], 0.0)
    bias = fold(bias_total[0:8])[0:1]
    bias_1 = rounded(bias)
    bias_2 = rounded(bias - bias_1)
    bias_3 = bias - bias_1 - bias_2
    block = block_of((1, 128))
    pieces = jnp.where(
        block == 0, bias_1, jnp.where(block == 1, bias_2, jnp.where(block == 2, bias_3, 0.0))
    )
    for z, h, out in outs:
        for p in range(2):
            wide[pl.ds(10 * z + 2 * p + h, KY, stride=20), :] = out[KY * p : KY * (p + 1)]
    for z in range(2):
        lines = [flat[4 * z + k : 4 * z + k + 1] for k in range(4)]
        lines = lines + [pieces, jnp.zeros((1, 128), F32)]
        for k, line in enumerate(lines):
            wide[pl.ds(10 * z + 4 + k, KY, stride=20), :] = jnp.broadcast_to(line, (KY, 128))
    send[...] = wide[...].astype(BF16)
    copies[1].wait()


def back_kernel(recv, forward, first, kept, share, held):
    real, imag = x_forward(recv, forward, held, 10)
    factor = mode_weight()
    real = rounded(real * factor)
    imag = rounded(imag * factor)
    kept[:KX] = real
    kept[KX:] = imag
    share[:KX] = paired(real, imag).astype(BF16)
    lines = [
        jnp.sum(held[pl.ds(4 + k, 128, stride=10), :], axis=0, keepdims=True) for k in range(5)
    ]
    total = jnp.concatenate(lines[:4], axis=0)
    bias = fold(lines[4])
    share[KX : KX + 16] = jnp.concatenate(
        [
            rounded(total),
            total - rounded(total),
            rounded(bias),
            bias - rounded(bias),
            jnp.zeros((6, 128), F32),
        ],
        axis=0,
    ).astype(BF16)
    share[KX + 16 :] = first[...]


def adjoint_kernel(kept, weight, inverse, shares, send, group, held, high, low):
    dre = kept[:KX]
    dim = kept[KX:]
    for t in range(8):
        cols = slice(128 * t, 128 * (t + 1))
        wre = weight[:, cols].astype(F32)
        wim = weight[:, 1024 + 128 * t : 1024 + 128 * (t + 1)].astype(F32)
        for k, term in ((0, dre * wre + dim * wim), (1, dim * wre - dre * wim)):
            top = term.astype(BF16)
            high[KX * k : KX * (k + 1), cols] = top
            low[KX * k : KX * (k + 1), cols] = (term - top.astype(F32)).astype(BF16)
    k = lax.broadcasted_iota(jnp.int32, (1024, 128), 0)
    lane = lax.broadcasted_iota(jnp.int32, (1024, 128), 1)
    gather = jnp.where((k >> 5) == (lane & 31), 1.0, 0.0).astype(BF16)
    back = rounded(nn(high[...], gather) + nn(low[...], gather))
    x_inverse(back[:KX], back[KX:], inverse, held, 4)
    send[...] = held[...].astype(BF16)
    start = 64 * lax.axis_index("core")
    left = block_of((64, 128)) < 2
    step = 2 * KX + 16
    for k, at in enumerate((KX + 16, 0)):
        one = shares[pl.ds(pl.multiple_of(at + start, 16), 64), :].astype(F32)
        two = shares[pl.ds(pl.multiple_of(step + at + start, 16), 64), :].astype(F32)
        group[64 * k : 64 * (k + 1)] = jnp.where(left, one, two).astype(BF16)
    group[128:144] = shares[KX : KX + 16]
    group[144:160] = shares[step + KX : step + KX + 16]


def final_kernel(
    recv, delta, local4, ytab, groups, field_grad, spectral_grad, local_grad, bias_grad,
    held, rows, out, tiles, out_local, out_bias, sems,
):
    held[...] = recv[...].astype(F32)
    copies = [
        pltpu.make_async_copy(rows, field_grad, sems.at[0]),
        pltpu.make_async_copy(out, spectral_grad, sems.at[1]),
        pltpu.make_async_copy(out_local, local_grad, sems.at[2]),
        pltpu.make_async_copy(out_bias, bias_grad, sems.at[3]),
    ]
    for k in range(4):
        z, h = k // 2, k % 2
        spectrum = jnp.concatenate(
            [held[pl.ds(4 * z + 2 * p + h, KY, stride=8), :] for p in range(2)], axis=0
        )
        left = jnp.concatenate([spectrum.T.astype(BF16), local4[...]], axis=1)
        for part in range(4):
            cols = slice(256 * part, 256 * (part + 1))
            right = jnp.concatenate([ytab[:, cols], delta[k, :, cols]], axis=0)
            rows[4 * h : 4 * h + 4, z, :, cols] = nn(left, right).astype(BF16).reshape(4, 32, 256)
    copies[0].start()
    lane = lax.broadcasted_iota(jnp.int32, (128, 1024), 1)
    k = lax.broadcasted_iota(jnp.int32, (128, 1024), 0)
    expand = jnp.where((lane >> 5) == k, 1.0, 0.0).astype(BF16)
    first = jnp.concatenate([groups[160 * g : 160 * g + 64] for g in range(4)], axis=0).astype(F32)
    turned = [first] + [pltpu.roll(first, 128 - 32 * b, 1) for b in range(1, 4)]
    compact = jnp.concatenate(turned, axis=0).astype(BF16)
    block = block_of((64, 128))
    for g in range(4):
        second = groups[160 * g + 64 : 160 * g + 128].astype(F32)
        for b in range(4):
            tiles[64 * (4 * g + b) : 64 * (4 * g + b + 1)] = fold(
                jnp.where(block == b, second, 0.0)
            )
    for pair in range(4):
        wide = nn(compact, expand[:, 256 * pair : 256 * (pair + 1)])
        for half in range(2):
            t = 2 * pair + half
            cols = slice(128 * half, 128 * (half + 1))
            real = jnp.zeros((64, 128), F32)
            imag = jnp.zeros((64, 128), F32)
            for g in range(4):
                for z in range(2):
                    b = 2 * z
                    ure = wide[256 * b + 64 * g : 256 * b + 64 * (g + 1), cols]
                    uim = wide[256 * (b + 1) + 64 * g : 256 * (b + 1) + 64 * (g + 1), cols]
                    dre = tiles[64 * (4 * g + b) : 64 * (4 * g + b + 1)]
                    dim = tiles[64 * (4 * g + b + 1) : 64 * (4 * g + b + 2)]
                    real = real + (ure * dre + uim * dim)
                    imag = imag + (ure * dim - uim * dre)
            out[:, 128 * t : 128 * (t + 1)] = real.astype(BF16)
            out[:, 1024 + 128 * t : 1024 + 128 * (t + 1)] = imag.astype(BF16)
    gscale = float((N * N * 8) ** -0.5)
    total = groups[128:160].astype(F32)
    for g in range(1, 4):
        total = total + groups[160 * g + 128 : 160 * g + 160].astype(F32)
    flat = jnp.concatenate(
        [total[0:4] + total[4:8], total[16:20] + total[20:24]], axis=0
    ) * gscale
    for q in range(4):
        out_local[pl.ds(q, 8, stride=4), :] = flat[:, 32 * q : 32 * (q + 1)]
    out_bias[...] = ((total[8:9] + total[9:10]) * gscale)[:, :32]
    for copy in copies[1:]:
        copy.start()
    for copy in copies:
        copy.wait()


def run(kernel, operands, outs, scratch, name, specs=None, out_specs=None):
    specs = specs or [VM] * len(operands)
    out_specs = out_specs or [VM] * len(outs)
    operands = [
        pltpu.with_memory_space_constraint(operand, pltpu.HBM) if spec is HBM else operand
        for operand, spec in zip(operands, specs)
    ]
    return pl.pallas_call(
        kernel,
        out_shape=[
            (pltpu.HBM if spec is HBM else jax.ShapeDtypeStruct)(*out)
            for out, spec in zip(outs, out_specs)
        ],
        in_specs=specs,
        out_specs=out_specs,
        scratch_shapes=scratch,
        compiler_params=pltpu.CompilerParams(vmem_limit_bytes=16 * 1024 * 1024),
        cost_estimate=pl.CostEstimate(
            flops=200_000_000, bytes_accessed=1 << 20, transcendentals=0
        ),
        name=name,
    )(*operands)


def exchange(values, *shape):
    blocks = values.reshape((128,) + shape)
    return lax.all_to_all(blocks, GX, 0, 0, tiled=True).reshape(values.shape)


def local(field, cotangent, spectral_weight, local_weight, bias):
    ytab, forward, inverse = (jnp.asarray(table) for table in tables())
    same = jnp.asarray(np.kron(np.eye(4), np.ones((C, C))).astype(ml_dtypes.bfloat16))
    local_in = jnp.tile(local_weight, (4, 4)) * same
    slab = ((512, 128), BF16)
    slab_wide = ((1280, 128), BF16)
    held = pltpu.VMEM((512, 128), F32)
    held_wide = pltpu.VMEM((1280, 128), F32)
    quarters = pltpu.VMEM((4, 4, C, N), BF16)

    (send,) = run(
        y_kernel,
        (field, ytab),
        [slab],
        [held, quarters, pltpu.VMEM((128, N), BF16), pltpu.SemaphoreType.DMA((5,))],
        "y_forward",
        [HBM, HBM],
    )
    recv = exchange(send, 4, 128)
    weight = lax.all_gather(spectral_weight, "core", axis=0, tiled=True)
    send, first = run(
        mix_kernel,
        (recv, weight, forward, inverse),
        [slab, ((KX, 128), BF16)],
        [held],
        "mix",
    )
    recv = exchange(send, 4, 128)
    send, delta = run(
        point_kernel,
        (recv, field, cotangent, local_weight, bias.reshape(1, C), ytab),
        [slab_wide, ((4, 128, N), BF16)],
        [
            held,
            held_wide,
            pltpu.VMEM((8, 2, C, N), BF16),
            pltpu.VMEM((4, 128, N), BF16),
            pltpu.VMEM((128, N), F32),
            pltpu.SemaphoreType.DMA((2,)),
        ],
        "pointwise",
        [VM, VM, HBM, VM, VM, VM],
        [VM, HBM],
    )
    recv = exchange(send, 5, 2, 128)
    second, share = run(
        back_kernel,
        (recv, forward, first),
        [((2 * KX, 128), F32), ((2 * KX + 16, 128), BF16)],
        [held_wide],
        "x_forward",
    )
    shares = lax.all_gather(share, "core", axis=0, tiled=True)
    send, group = run(
        adjoint_kernel,
        (second, weight, inverse, shares),
        [slab, ((160, 128), BF16)],
        [held, pltpu.VMEM((256, 1024), BF16), pltpu.VMEM((256, 1024), BF16)],
        "adjoint",
    )
    recv = exchange(send, 4, 128)
    groups = lax.all_gather(group, "gz", axis=0, tiled=True)
    field_grad, spectral_grad, local_grad, bias_grad = run(
        final_kernel,
        (recv, delta, local_in, ytab, groups),
        [((8, 2, C, N), BF16), ((64, 2048), BF16), ((C, C), F32), ((1, C), F32)],
        [
            held,
            pltpu.VMEM((8, 2, C, N), BF16),
            pltpu.VMEM((64, 2048), BF16),
            pltpu.VMEM((1024, 128), F32),
            pltpu.VMEM((C, C), F32),
            pltpu.VMEM((1, C), F32),
            pltpu.SemaphoreType.DMA((4,)),
        ],
        "final",
        None,
        [HBM] * 4,
    )
    return field_grad, spectral_grad, local_grad, bias_grad.reshape(C)


def solution(mesh):
    fine = Mesh(mesh.devices.reshape(8, 8, 2, 4), GX + ("gz",))
    cells = P(GX, "gz", None, None)
    return jax.shard_map(
        local,
        mesh=fine,
        in_specs=(cells, cells, P(GX, None), P(), P()),
        out_specs=(cells, P(GX, None), P(), P()),
        check_vma=False,
    )
```

```python
import jax
import jax.numpy as jnp
import ml_dtypes
import numpy as np
from jax import lax
from jax.experimental import pallas as pl
from jax.experimental.pallas import tpu as pltpu
from jax.sharding import Mesh
from jax.sharding import PartitionSpec as P

KX = 128
KY = 64
C = 32
N = 1024
F32 = jnp.float32
BF16 = jnp.bfloat16
GX = ("y", "z", "core")
VM = pl.BlockSpec(memory_space=pltpu.VMEM)
HBM = pl.BlockSpec(memory_space=pltpu.HBM)
COST = {"mix": 800_000_000}


def angles(freq, pos):
    product = (freq[:, None].astype(np.int64) * pos[None, :].astype(np.int64)) % N
    angle = product.astype(np.float32) * np.float32(2.0 * np.pi / N)
    return np.cos(angle).astype(np.float32), np.sin(angle).astype(np.float32)


def tables():
    ycos, ysin = angles(np.arange(KY), np.arange(N))
    ytab = np.concatenate([ycos, -ysin], axis=0).astype(ml_dtypes.bfloat16)
    ytab = (ytab.astype(np.float32) / 32.0).astype(ml_dtypes.bfloat16)
    j = np.arange(KX)
    freq = np.where(j < KX // 2, j, j - KX)
    r, h, d = np.meshgrid(np.arange(4), np.arange(2), np.arange(128), indexing="ij")
    xcos, xsin = angles(freq, (8 * d + 4 * h + r).reshape(-1))
    forward = np.concatenate([xcos, xsin], axis=0).astype(ml_dtypes.bfloat16)
    inverse = forward.reshape(2 * KX, 4, 256).transpose(2, 1, 0).reshape(256, 1024)
    return ytab, forward, np.ascontiguousarray(inverse)


def nt(a, b):
    return lax.dot_general(a, b, (((1,), (1,)), ((), ())), preferred_element_type=F32)


def nn(a, b):
    return jnp.dot(a, b, preferred_element_type=F32)


def block_of(shape):
    return (lax.broadcasted_iota(jnp.int32, shape, 1) >> 5) & 3


def fold(v):
    v = v + pltpu.roll(v, 64, 1)
    return v + pltpu.roll(v, 32, 1)


def spread(base):
    block = block_of(base.shape)
    return jnp.concatenate([jnp.where(block == r, base, 0.0) for r in range(4)], axis=0).astype(BF16)


def rounded(v):
    return v.astype(BF16).astype(F32)


def mode_weight():
    first = (lax.axis_index("y") + lax.axis_index("z")) == 0
    return jnp.where(first, 1.0, 2.0).astype(F32)


def x_forward(recv, table, held, stride):
    held[...] = recv[...].astype(F32)
    parts = [
        jnp.concatenate([held[pl.ds(2 * p + h, 128, stride=stride), :] for h in range(2)], axis=0)
        for p in range(2)
    ]
    out = nn(table[...], spread(jnp.concatenate(parts, axis=1)))
    real = out[:KX, :128] + out[KX:, 128:]
    imag = out[:KX, 128:] - out[KX:, :128]
    return fold(real) * (1.0 / 32.0), fold(imag) * (1.0 / 32.0)


def paired(real, imag):
    return jnp.where((block_of(real.shape) & 1) == 0, real, imag)


def x_inverse(real, imag, table, held, stride):
    base = jnp.concatenate(
        [jnp.concatenate([real, imag], axis=1), jnp.concatenate([-imag, real], axis=1)], axis=0
    )
    out = nn(table[...], spread(base)) * (1.0 / 32.0)
    for p in range(2):
        for h in range(2):
            held[pl.ds(2 * p + h, 128, stride=stride), :] = out[
                128 * h : 128 * (h + 1), 128 * p : 128 * (p + 1)
            ]


def y_kernel(field, ytab, send, held, rows, table, sems):
    copies = [pltpu.make_async_copy(ytab, table, sems.at[4])]
    for k in range(4):
        part = field.at[pl.ds(4 * (k % 2), 4), k // 2]
        copies.append(pltpu.make_async_copy(part, rows.at[k], sems.at[k]))
    for copy in copies:
        copy.start()
    for k in range(4):
        z, h = k // 2, k % 2
        if h == 0:
            for copy in copies[3 * z : 3 + 2 * z]:
                copy.wait()
        out = nt(table[...], rows[k].reshape(128, N))
        for p in range(2):
            held[pl.ds(4 * z + 2 * p + h, KY, stride=8), :] = out[KY * p : KY * (p + 1)]
    send[...] = held[...].astype(BF16)


def mix_kernel(recv, weight, forward, inverse, bias, send, kept, bias_row, held, sem):
    copy = pltpu.make_async_copy(bias, bias_row, sem.at[0])
    copy.start()
    real, imag = x_forward(recv, forward, held, 4)
    real = rounded(real)
    imag = rounded(imag)
    kept[...] = paired(real, imag).astype(BF16)
    k = lax.broadcasted_iota(jnp.int32, (128, 1024), 0)
    lane = lax.broadcasted_iota(jnp.int32, (128, 1024), 1)
    expand = jnp.where((lane >> 5) == k, 1.0, 0.0).astype(BF16)
    wide = nn(jnp.concatenate([real, imag], axis=0).astype(BF16), expand)
    vre = jnp.zeros((KX, 128), F32)
    vim = jnp.zeros((KX, 128), F32)
    for t in range(8):
        wre = weight[:, 128 * t : 128 * (t + 1)].astype(F32)
        wim = weight[:, 1024 + 128 * t : 1024 + 128 * (t + 1)].astype(F32)
        ure = wide[:KX, 128 * t : 128 * (t + 1)]
        uim = wide[KX:, 128 * t : 128 * (t + 1)]
        vre = vre + (ure * wre - uim * wim)
        vim = vim + (ure * wim + uim * wre)
    factor = mode_weight()
    x_inverse(rounded(fold(vre) * factor), rounded(fold(vim) * factor), inverse, held, 4)
    send[...] = held[...].astype(BF16)
    copy.wait()


def point_kernel(recv, field, cotangent, local, bias, ytab, send, delta, held, wide):
    held[...] = recv[...].astype(F32)
    row = lax.broadcasted_iota(jnp.int32, (128, C), 0)
    same = jnp.where((row & 31) == lax.broadcasted_iota(jnp.int32, (128, C), 1), 1.0, 0.0)
    bias4 = jnp.sum(same * bias[...], axis=1, keepdims=True)
    picks = same.astype(BF16)
    local4 = nt(nt(picks, local[...]).astype(BF16), picks)
    row = lax.broadcasted_iota(jnp.int32, (128, 128), 0)
    local4 = jnp.where((row >> 5) == block_of((128, 128)), local4, 0.0).astype(BF16)
    ones = jnp.ones((16, N), BF16)
    total = jnp.zeros((144, 128), F32)
    outs = []
    for k in range(4):
        z, h = k // 2, k % 2
        spectrum = jnp.concatenate(
            [held[pl.ds(4 * z + 2 * p + h, KY, stride=8), :] for p in range(2)], axis=0
        )
        left = jnp.concatenate([spectrum.T.astype(BF16), local4], axis=1)
        rows = field[4 * h : 4 * h + 4, z].reshape(128, N)
        cot = cotangent[4 * h : 4 * h + 4, z].reshape(128, N)
        for part in range(4):
            cols = slice(256 * part, 256 * (part + 1))
            right = jnp.concatenate([ytab[:, cols], rows[:, cols]], axis=0)
            pre = nn(left, right) + bias4
            sig = 0.5 * jnp.tanh(0.5 * pre) + 0.5
            slope = sig * (1.0 + pre * (1.0 - sig))
            delta[k, :, cols] = (cot[:, cols].astype(F32) * slope).astype(BF16)
    for k in range(4):
        z, h = k // 2, k % 2
        rows = field[4 * h : 4 * h + 4, z].reshape(128, N)
        out = nt(jnp.concatenate([ytab[...], rows, ones], axis=0), delta[k])
        outs.append((z, h, out[:128]))
        total = total + out[128:]
    bias_total = total[128:]
    block = block_of((32, 128))
    diag = jnp.zeros((32, 128), F32)
    for r in range(4):
        diag = diag + jnp.where(block == r, total[32 * r : 32 * (r + 1)], 0.0)
    held[0:32, :] = fold(diag)
    block = block_of((8, 128))
    flat = jnp.zeros((8, 128), F32)
    for q in range(4):
        flat = flat + jnp.where(block == q, held[pl.ds(q, 8, stride=4), :], 0.0)
    bias = fold(bias_total[0:8])[0:1]
    bias_1 = rounded(bias)
    bias_2 = rounded(bias - bias_1)
    bias_3 = bias - bias_1 - bias_2
    block = block_of((1, 128))
    pieces = jnp.where(
        block == 0, bias_1, jnp.where(block == 1, bias_2, jnp.where(block == 2, bias_3, 0.0))
    )
    for z, h, out in outs:
        for p in range(2):
            wide[pl.ds(10 * z + 2 * p + h, KY, stride=20), :] = out[KY * p : KY * (p + 1)]
    for z in range(2):
        lines = [flat[4 * z + k : 4 * z + k + 1] for k in range(4)]
        lines = lines + [pieces, jnp.zeros((1, 128), F32)]
        for k, line in enumerate(lines):
            wide[pl.ds(10 * z + 4 + k, KY, stride=20), :] = jnp.broadcast_to(line, (KY, 128))
    send[...] = wide[...].astype(BF16)


def back_kernel(recv, forward, first, kept, share, held):
    real, imag = x_forward(recv, forward, held, 10)
    factor = mode_weight()
    real = rounded(real * factor)
    imag = rounded(imag * factor)
    kept[:KX] = real
    kept[KX:] = imag
    share[:KX] = paired(real, imag).astype(BF16)
    lines = [
        jnp.sum(held[pl.ds(4 + k, 128, stride=10), :], axis=0, keepdims=True) for k in range(5)
    ]
    total = jnp.concatenate(lines[:4], axis=0)
    bias = fold(lines[4])
    share[KX : KX + 16] = jnp.concatenate(
        [
            rounded(total),
            total - rounded(total),
            rounded(bias),
            bias - rounded(bias),
            jnp.zeros((6, 128), F32),
        ],
        axis=0,
    ).astype(BF16)
    share[KX + 16 :] = first[...]


def adjoint_kernel(kept, weight, inverse, shares, send, group, held, high, low):
    dre = kept[:KX]
    dim = kept[KX:]
    for t in range(8):
        cols = slice(128 * t, 128 * (t + 1))
        wre = weight[:, cols].astype(F32)
        wim = weight[:, 1024 + 128 * t : 1024 + 128 * (t + 1)].astype(F32)
        for k, term in ((0, dre * wre + dim * wim), (1, dim * wre - dre * wim)):
            top = term.astype(BF16)
            high[KX * k : KX * (k + 1), cols] = top
            low[KX * k : KX * (k + 1), cols] = (term - top.astype(F32)).astype(BF16)
    k = lax.broadcasted_iota(jnp.int32, (1024, 128), 0)
    lane = lax.broadcasted_iota(jnp.int32, (1024, 128), 1)
    gather = jnp.where((k >> 5) == (lane & 31), 1.0, 0.0).astype(BF16)
    back = rounded(nn(high[...], gather) + nn(low[...], gather))
    x_inverse(back[:KX], back[KX:], inverse, held, 4)
    send[...] = held[...].astype(BF16)
    start = 64 * lax.axis_index("core")
    left = block_of((64, 128)) < 2
    step = 2 * KX + 16
    for k, at in enumerate((KX + 16, 0)):
        one = shares[pl.ds(pl.multiple_of(at + start, 16), 64), :].astype(F32)
        two = shares[pl.ds(pl.multiple_of(step + at + start, 16), 64), :].astype(F32)
        group[64 * k : 64 * (k + 1)] = jnp.where(left, one, two).astype(BF16)
    group[128:144] = shares[KX : KX + 16]
    group[144:160] = shares[step + KX : step + KX + 16]


def final_kernel(
    recv, delta, local4, ytab, groups, field_grad, spectral_grad, local_grad, bias_grad,
    held, rows, out, tiles, out_local, out_bias, sems,
):
    held[...] = recv[...].astype(F32)
    copies = [
        pltpu.make_async_copy(rows, field_grad, sems.at[0]),
        pltpu.make_async_copy(out, spectral_grad, sems.at[1]),
        pltpu.make_async_copy(out_local, local_grad, sems.at[2]),
        pltpu.make_async_copy(out_bias, bias_grad, sems.at[3]),
    ]
    for k in range(4):
        z, h = k // 2, k % 2
        spectrum = jnp.concatenate(
            [held[pl.ds(4 * z + 2 * p + h, KY, stride=8), :] for p in range(2)], axis=0
        )
        left = jnp.concatenate([spectrum.T.astype(BF16), local4[...]], axis=1)
        for part in range(4):
            cols = slice(256 * part, 256 * (part + 1))
            right = jnp.concatenate([ytab[:, cols], delta[k, :, cols]], axis=0)
            rows[4 * h : 4 * h + 4, z, :, cols] = nn(left, right).astype(BF16).reshape(4, 32, 256)
    copies[0].start()
    lane = lax.broadcasted_iota(jnp.int32, (128, 1024), 1)
    k = lax.broadcasted_iota(jnp.int32, (128, 1024), 0)
    expand = jnp.where((lane >> 5) == k, 1.0, 0.0).astype(BF16)
    first = jnp.concatenate([groups[160 * g : 160 * g + 64] for g in range(4)], axis=0).astype(F32)
    turned = [first] + [pltpu.roll(first, 128 - 32 * b, 1) for b in range(1, 4)]
    compact = jnp.concatenate(turned, axis=0).astype(BF16)
    block = block_of((64, 128))
    for g in range(4):
        second = groups[160 * g + 64 : 160 * g + 128].astype(F32)
        for b in range(4):
            tiles[64 * (4 * g + b) : 64 * (4 * g + b + 1)] = fold(
                jnp.where(block == b, second, 0.0)
            )
    for pair in range(4):
        wide = nn(compact, expand[:, 256 * pair : 256 * (pair + 1)])
        for half in range(2):
            t = 2 * pair + half
            cols = slice(128 * half, 128 * (half + 1))
            real = jnp.zeros((64, 128), F32)
            imag = jnp.zeros((64, 128), F32)
            for g in range(4):
                for z in range(2):
                    b = 2 * z
                    ure = wide[256 * b + 64 * g : 256 * b + 64 * (g + 1), cols]
                    uim = wide[256 * (b + 1) + 64 * g : 256 * (b + 1) + 64 * (g + 1), cols]
                    dre = tiles[64 * (4 * g + b) : 64 * (4 * g + b + 1)]
                    dim = tiles[64 * (4 * g + b + 1) : 64 * (4 * g + b + 2)]
                    real = real + (ure * dre + uim * dim)
                    imag = imag + (ure * dim - uim * dre)
            out[:, 128 * t : 128 * (t + 1)] = real.astype(BF16)
            out[:, 1024 + 128 * t : 1024 + 128 * (t + 1)] = imag.astype(BF16)
    gscale = float((N * N * 8) ** -0.5)
    total = groups[128:160].astype(F32)
    for g in range(1, 4):
        total = total + groups[160 * g + 128 : 160 * g + 160].astype(F32)
    flat = jnp.concatenate(
        [total[0:4] + total[4:8], total[16:20] + total[20:24]], axis=0
    ) * gscale
    for q in range(4):
        out_local[pl.ds(q, 8, stride=4), :] = flat[:, 32 * q : 32 * (q + 1)]
    out_bias[...] = ((total[8:9] + total[9:10]) * gscale)[:, :32]
    for copy in copies[1:]:
        copy.start()
    for copy in copies:
        copy.wait()


def run(kernel, operands, outs, scratch, name, specs=None, out_specs=None):
    specs = specs or [VM] * len(operands)
    out_specs = out_specs or [VM] * len(outs)
    operands = [
        pltpu.with_memory_space_constraint(operand, pltpu.HBM) if spec is HBM else operand
        for operand, spec in zip(operands, specs)
    ]
    return pl.pallas_call(
        kernel,
        out_shape=[
            (pltpu.HBM if spec is HBM else jax.ShapeDtypeStruct)(*out)
            for out, spec in zip(outs, out_specs)
        ],
        in_specs=specs,
        out_specs=out_specs,
        scratch_shapes=scratch,
        compiler_params=pltpu.CompilerParams(vmem_limit_bytes=16 * 1024 * 1024),
        cost_estimate=pl.CostEstimate(
            flops=COST.get(name, 200_000_000), bytes_accessed=1 << 20, transcendentals=0
        ),
        name=name,
    )(*operands)


def exchange(values, *shape):
    blocks = values.reshape((128,) + shape)
    return lax.all_to_all(blocks, GX, 0, 0, tiled=True).reshape(values.shape)


def local(field, cotangent, spectral_weight, local_weight, bias):
    ytab, forward, inverse = (jnp.asarray(table) for table in tables())
    same = jnp.asarray(np.kron(np.eye(4), np.ones((C, C))).astype(ml_dtypes.bfloat16))
    local_in = jnp.tile(local_weight, (4, 4)) * same
    slab = ((512, 128), BF16)
    slab_wide = ((1280, 128), BF16)
    held = pltpu.VMEM((512, 128), F32)
    held_wide = pltpu.VMEM((1280, 128), F32)
    quarters = pltpu.VMEM((4, 4, C, N), BF16)

    (send,) = run(
        y_kernel,
        (field, ytab),
        [slab],
        [held, quarters, pltpu.VMEM((128, N), BF16), pltpu.SemaphoreType.DMA((5,))],
        "y_forward",
        [HBM, HBM],
    )
    recv = exchange(send, 4, 128)
    weight = lax.all_gather(spectral_weight, "core", axis=0, tiled=True)
    send, first, bias_row = run(
        mix_kernel,
        (recv, weight, forward, inverse, bias.reshape(1, C)),
        [slab, ((KX, 128), BF16), ((1, C), F32)],
        [held, pltpu.SemaphoreType.DMA((1,))],
        "mix",
        [VM, VM, VM, VM, HBM],
    )
    recv = exchange(send, 4, 128)
    send, delta = run(
        point_kernel,
        (recv, field, cotangent, local_weight, bias_row, ytab),
        [slab_wide, ((4, 128, N), BF16)],
        [
            held,
            held_wide,
        ],
        "pointwise",
    )
    recv = exchange(send, 5, 2, 128)
    second, share = run(
        back_kernel,
        (recv, forward, first),
        [((2 * KX, 128), F32), ((2 * KX + 16, 128), BF16)],
        [held_wide],
        "x_forward",
    )
    shares = lax.all_gather(share, "core", axis=0, tiled=True)
    send, group = run(
        adjoint_kernel,
        (second, weight, inverse, shares),
        [slab, ((160, 128), BF16)],
        [held, pltpu.VMEM((256, 1024), BF16), pltpu.VMEM((256, 1024), BF16)],
        "adjoint",
    )
    recv = exchange(send, 4, 128)
    for pairs in ([[0, 1], [2, 3]], [[0, 3], [1, 2]]):
        group = lax.all_gather(group, "gz", axis=0, tiled=True, axis_index_groups=pairs)
    field_grad, spectral_grad, local_grad, bias_grad = run(
        final_kernel,
        (recv, delta, local_in, ytab, group),
        [((8, 2, C, N), BF16), ((64, 2048), BF16), ((C, C), F32), ((1, C), F32)],
        [
            held,
            pltpu.VMEM((8, 2, C, N), BF16),
            pltpu.VMEM((64, 2048), BF16),
            pltpu.VMEM((1024, 128), F32),
            pltpu.VMEM((C, C), F32),
            pltpu.VMEM((1, C), F32),
            pltpu.SemaphoreType.DMA((4,)),
        ],
        "final",
        None,
        [HBM] * 4,
    )
    return field_grad, spectral_grad, local_grad, bias_grad.reshape(C)


def solution(mesh):
    fine = Mesh(mesh.devices.reshape(8, 8, 2, 4), GX + ("gz",))
    cells = P(GX, "gz", None, None)
    return jax.shard_map(
        local,
        mesh=fine,
        in_specs=(cells, cells, P(GX, None), P(), P()),
        out_specs=(cells, P(GX, None), P(), P()),
        check_vma=False,
    )
```

```python
import jax
import jax.numpy as jnp
import ml_dtypes
import numpy as np
from jax import lax
from jax.experimental import pallas as pl
from jax.experimental.pallas import tpu as pltpu
from jax.sharding import Mesh
from jax.sharding import PartitionSpec as P

KX = 128
KY = 64
C = 32
N = 1024
F32 = jnp.float32
BF16 = jnp.bfloat16
GX = ("y", "z", "core")
VM = pl.BlockSpec(memory_space=pltpu.VMEM)
HBM = pl.BlockSpec(memory_space=pltpu.HBM)
COST = {"mix": 800_000_000}


def angles(freq, pos):
    product = (freq[:, None].astype(np.int64) * pos[None, :].astype(np.int64)) % N
    angle = product.astype(np.float32) * np.float32(2.0 * np.pi / N)
    return np.cos(angle).astype(np.float32), np.sin(angle).astype(np.float32)


def tables():
    ycos, ysin = angles(np.arange(KY), np.arange(N))
    ytab = np.concatenate([ycos, -ysin], axis=0).astype(ml_dtypes.bfloat16)
    ytab = (ytab.astype(np.float32) / 32.0).astype(ml_dtypes.bfloat16)
    j = np.arange(KX)
    freq = np.where(j < KX // 2, j, j - KX)
    r, h, d = np.meshgrid(np.arange(4), np.arange(2), np.arange(128), indexing="ij")
    xcos, xsin = angles(freq, (8 * d + 4 * h + r).reshape(-1))
    forward = np.concatenate([xcos, xsin], axis=0).astype(ml_dtypes.bfloat16)
    inverse = forward.reshape(2 * KX, 4, 256).transpose(2, 1, 0).reshape(256, 1024)
    return ytab, forward, np.ascontiguousarray(inverse)


def nt(a, b):
    return lax.dot_general(a, b, (((1,), (1,)), ((), ())), preferred_element_type=F32)


def nn(a, b):
    return jnp.dot(a, b, preferred_element_type=F32)


def block_of(shape):
    return (lax.broadcasted_iota(jnp.int32, shape, 1) >> 5) & 3


def fold(v):
    v = v + pltpu.roll(v, 64, 1)
    return v + pltpu.roll(v, 32, 1)


def spread(base):
    block = block_of(base.shape)
    return jnp.concatenate([jnp.where(block == r, base, 0.0) for r in range(4)], axis=0).astype(BF16)


def rounded(v):
    return v.astype(BF16).astype(F32)


def mode_weight():
    first = (lax.axis_index("y") + lax.axis_index("z")) == 0
    return jnp.where(first, 1.0, 2.0).astype(F32)


def x_forward(recv, table, held, stride):
    held[...] = recv[...].astype(F32)
    parts = [
        jnp.concatenate([held[pl.ds(2 * p + h, 128, stride=stride), :] for h in range(2)], axis=0)
        for p in range(2)
    ]
    out = nn(table[...], spread(jnp.concatenate(parts, axis=1)))
    real = out[:KX, :128] + out[KX:, 128:]
    imag = out[:KX, 128:] - out[KX:, :128]
    return fold(real) * (1.0 / 32.0), fold(imag) * (1.0 / 32.0)


def paired(real, imag):
    return jnp.where((block_of(real.shape) & 1) == 0, real, imag)


def x_inverse(real, imag, table, held, stride):
    base = jnp.concatenate(
        [jnp.concatenate([real, imag], axis=1), jnp.concatenate([-imag, real], axis=1)], axis=0
    )
    out = nn(table[...], spread(base)) * (1.0 / 32.0)
    for p in range(2):
        for h in range(2):
            held[pl.ds(2 * p + h, 128, stride=stride), :] = out[
                128 * h : 128 * (h + 1), 128 * p : 128 * (p + 1)
            ]


def y_kernel(field, ytab, bias, local, send, bias_row, local_near, held, rows, table, sems):
    copies = [pltpu.make_async_copy(ytab, table, sems.at[4])]
    for k in range(4):
        part = field.at[pl.ds(4 * (k % 2), 4), k // 2]
        copies.append(pltpu.make_async_copy(part, rows.at[k], sems.at[k]))
    copies.append(pltpu.make_async_copy(bias, bias_row, sems.at[5]))
    copies.append(pltpu.make_async_copy(local, local_near, sems.at[6]))
    for copy in copies:
        copy.start()
    for k in range(4):
        z, h = k // 2, k % 2
        if h == 0:
            for copy in copies[3 * z : 3 + 4 * z]:
                copy.wait()
        out = nt(table[...], rows[k].reshape(128, N))
        for p in range(2):
            held[pl.ds(4 * z + 2 * p + h, KY, stride=8), :] = out[KY * p : KY * (p + 1)]
    send[...] = held[...].astype(BF16)


def mix_kernel(recv, weight, forward, inverse, send, kept, held):
    real, imag = x_forward(recv, forward, held, 4)
    real = rounded(real)
    imag = rounded(imag)
    kept[...] = paired(real, imag).astype(BF16)
    k = lax.broadcasted_iota(jnp.int32, (128, 1024), 0)
    lane = lax.broadcasted_iota(jnp.int32, (128, 1024), 1)
    expand = jnp.where((lane >> 5) == k, 1.0, 0.0).astype(BF16)
    wide = nn(jnp.concatenate([real, imag], axis=0).astype(BF16), expand)
    vre = jnp.zeros((KX, 128), F32)
    vim = jnp.zeros((KX, 128), F32)
    for t in range(8):
        wre = weight[:, 128 * t : 128 * (t + 1)].astype(F32)
        wim = weight[:, 1024 + 128 * t : 1024 + 128 * (t + 1)].astype(F32)
        ure = wide[:KX, 128 * t : 128 * (t + 1)]
        uim = wide[KX:, 128 * t : 128 * (t + 1)]
        vre = vre + (ure * wre - uim * wim)
        vim = vim + (ure * wim + uim * wre)
    factor = mode_weight()
    x_inverse(rounded(fold(vre) * factor), rounded(fold(vim) * factor), inverse, held, 4)
    send[...] = held[...].astype(BF16)


def repeats():
    row = lax.broadcasted_iota(jnp.int32, (128, C), 0)
    return jnp.where((row & 31) == lax.broadcasted_iota(jnp.int32, (128, C), 1), 1.0, 0.0)


def blocks(tall, picks):
    row = lax.broadcasted_iota(jnp.int32, (128, 128), 0)
    wide = nt(tall.astype(BF16), picks)
    return jnp.where((row >> 5) == block_of((128, 128)), wide, 0.0).astype(BF16)


def point_kernel(recv, field, cotangent, local, bias, ytab, send, delta, held, wide):
    held[...] = recv[...].astype(F32)
    same = repeats()
    bias4 = jnp.sum(same * bias[...], axis=1, keepdims=True)
    picks = same.astype(BF16)
    local4 = blocks(nt(picks, local[...]), picks)
    ones = jnp.ones((16, N), BF16)
    total = jnp.zeros((144, 128), F32)
    outs = []
    for k in range(4):
        z, h = k // 2, k % 2
        spectrum = jnp.concatenate(
            [held[pl.ds(4 * z + 2 * p + h, KY, stride=8), :] for p in range(2)], axis=0
        )
        left = jnp.concatenate([spectrum.T.astype(BF16), local4], axis=1)
        rows = field[4 * h : 4 * h + 4, z].reshape(128, N)
        cot = cotangent[4 * h : 4 * h + 4, z].reshape(128, N)
        for part in range(4):
            cols = slice(256 * part, 256 * (part + 1))
            right = jnp.concatenate([ytab[:, cols], rows[:, cols]], axis=0)
            pre = nn(left, right) + bias4
            sig = 0.5 * jnp.tanh(0.5 * pre) + 0.5
            slope = sig * (1.0 + pre * (1.0 - sig))
            delta[k, :, cols] = (cot[:, cols].astype(F32) * slope).astype(BF16)
    for k in range(4):
        z, h = k // 2, k % 2
        rows = field[4 * h : 4 * h + 4, z].reshape(128, N)
        out = nt(jnp.concatenate([ytab[...], rows, ones], axis=0), delta[k])
        outs.append((z, h, out[:128]))
        total = total + out[128:]
    bias_total = total[128:]
    block = block_of((32, 128))
    diag = jnp.zeros((32, 128), F32)
    for r in range(4):
        diag = diag + jnp.where(block == r, total[32 * r : 32 * (r + 1)], 0.0)
    held[0:32, :] = fold(diag)
    block = block_of((8, 128))
    flat = jnp.zeros((8, 128), F32)
    for q in range(4):
        flat = flat + jnp.where(block == q, held[pl.ds(q, 8, stride=4), :], 0.0)
    bias = fold(bias_total[0:8])[0:1]
    bias_1 = rounded(bias)
    bias_2 = rounded(bias - bias_1)
    bias_3 = bias - bias_1 - bias_2
    block = block_of((1, 128))
    pieces = jnp.where(
        block == 0, bias_1, jnp.where(block == 1, bias_2, jnp.where(block == 2, bias_3, 0.0))
    )
    for z, h, out in outs:
        for p in range(2):
            wide[pl.ds(10 * z + 2 * p + h, KY, stride=20), :] = out[KY * p : KY * (p + 1)]
    for z in range(2):
        lines = [flat[4 * z + k : 4 * z + k + 1] for k in range(4)]
        lines = lines + [pieces, jnp.zeros((1, 128), F32)]
        for k, line in enumerate(lines):
            wide[pl.ds(10 * z + 4 + k, KY, stride=20), :] = jnp.broadcast_to(line, (KY, 128))
    send[...] = wide[...].astype(BF16)


def back_kernel(recv, forward, first, kept, share, held):
    real, imag = x_forward(recv, forward, held, 10)
    factor = mode_weight()
    real = rounded(real * factor)
    imag = rounded(imag * factor)
    kept[:KX] = real
    kept[KX:] = imag
    share[:KX] = paired(real, imag).astype(BF16)
    lines = [
        jnp.sum(held[pl.ds(4 + k, 128, stride=10), :], axis=0, keepdims=True) for k in range(5)
    ]
    total = jnp.concatenate(lines[:4], axis=0)
    bias = fold(lines[4])
    share[KX : KX + 16] = jnp.concatenate(
        [
            rounded(total),
            total - rounded(total),
            rounded(bias),
            bias - rounded(bias),
            jnp.zeros((6, 128), F32),
        ],
        axis=0,
    ).astype(BF16)
    share[KX + 16 :] = first[...]


def adjoint_kernel(kept, weight, inverse, shares, send, group, held, high, low):
    dre = kept[:KX]
    dim = kept[KX:]
    for t in range(8):
        cols = slice(128 * t, 128 * (t + 1))
        wre = weight[:, cols].astype(F32)
        wim = weight[:, 1024 + 128 * t : 1024 + 128 * (t + 1)].astype(F32)
        for k, term in ((0, dre * wre + dim * wim), (1, dim * wre - dre * wim)):
            top = term.astype(BF16)
            high[KX * k : KX * (k + 1), cols] = top
            low[KX * k : KX * (k + 1), cols] = (term - top.astype(F32)).astype(BF16)
    k = lax.broadcasted_iota(jnp.int32, (1024, 128), 0)
    lane = lax.broadcasted_iota(jnp.int32, (1024, 128), 1)
    gather = jnp.where((k >> 5) == (lane & 31), 1.0, 0.0).astype(BF16)
    back = rounded(nn(high[...], gather) + nn(low[...], gather))
    x_inverse(back[:KX], back[KX:], inverse, held, 4)
    send[...] = held[...].astype(BF16)
    start = 64 * lax.axis_index("core")
    left = block_of((64, 128)) < 2
    step = 2 * KX + 16
    for k, at in enumerate((KX + 16, 0)):
        one = shares[pl.ds(pl.multiple_of(at + start, 16), 64), :].astype(F32)
        two = shares[pl.ds(pl.multiple_of(step + at + start, 16), 64), :].astype(F32)
        group[64 * k : 64 * (k + 1)] = jnp.where(left, one, two).astype(BF16)
    group[128:144] = shares[KX : KX + 16]
    group[144:160] = shares[step + KX : step + KX + 16]


def final_kernel(
    recv, delta, local, ytab, groups, field_grad, spectral_grad, local_grad, bias_grad,
    held, rows, out, tiles, out_local, out_bias, sems,
):
    held[...] = recv[...].astype(F32)
    picks = repeats().astype(BF16)
    local4 = blocks(nn(picks, local[...]), picks)
    copies = [
        pltpu.make_async_copy(rows, field_grad, sems.at[0]),
        pltpu.make_async_copy(out, spectral_grad, sems.at[1]),
        pltpu.make_async_copy(out_local, local_grad, sems.at[2]),
        pltpu.make_async_copy(out_bias, bias_grad, sems.at[3]),
    ]
    for k in range(4):
        z, h = k // 2, k % 2
        spectrum = jnp.concatenate(
            [held[pl.ds(4 * z + 2 * p + h, KY, stride=8), :] for p in range(2)], axis=0
        )
        left = jnp.concatenate([spectrum.T.astype(BF16), local4], axis=1)
        for part in range(4):
            cols = slice(256 * part, 256 * (part + 1))
            right = jnp.concatenate([ytab[:, cols], delta[k, :, cols]], axis=0)
            rows[4 * h : 4 * h + 4, z, :, cols] = nn(left, right).astype(BF16).reshape(4, 32, 256)
    copies[0].start()
    lane = lax.broadcasted_iota(jnp.int32, (128, 1024), 1)
    k = lax.broadcasted_iota(jnp.int32, (128, 1024), 0)
    expand = jnp.where((lane >> 5) == k, 1.0, 0.0).astype(BF16)
    first = jnp.concatenate([groups[160 * g : 160 * g + 64] for g in range(4)], axis=0).astype(F32)
    turned = [first] + [pltpu.roll(first, 128 - 32 * b, 1) for b in range(1, 4)]
    compact = jnp.concatenate(turned, axis=0).astype(BF16)
    block = block_of((64, 128))
    for g in range(4):
        second = groups[160 * g + 64 : 160 * g + 128].astype(F32)
        for b in range(4):
            tiles[64 * (4 * g + b) : 64 * (4 * g + b + 1)] = fold(
                jnp.where(block == b, second, 0.0)
            )
    for pair in range(4):
        wide = nn(compact, expand[:, 256 * pair : 256 * (pair + 1)])
        for half in range(2):
            t = 2 * pair + half
            cols = slice(128 * half, 128 * (half + 1))
            real = jnp.zeros((64, 128), F32)
            imag = jnp.zeros((64, 128), F32)
            for g in range(4):
                for z in range(2):
                    b = 2 * z
                    ure = wide[256 * b + 64 * g : 256 * b + 64 * (g + 1), cols]
                    uim = wide[256 * (b + 1) + 64 * g : 256 * (b + 1) + 64 * (g + 1), cols]
                    dre = tiles[64 * (4 * g + b) : 64 * (4 * g + b + 1)]
                    dim = tiles[64 * (4 * g + b + 1) : 64 * (4 * g + b + 2)]
                    real = real + (ure * dre + uim * dim)
                    imag = imag + (ure * dim - uim * dre)
            out[:, 128 * t : 128 * (t + 1)] = real.astype(BF16)
            out[:, 1024 + 128 * t : 1024 + 128 * (t + 1)] = imag.astype(BF16)
    gscale = float((N * N * 8) ** -0.5)
    total = groups[128:160].astype(F32)
    for g in range(1, 4):
        total = total + groups[160 * g + 128 : 160 * g + 160].astype(F32)
    flat = jnp.concatenate(
        [total[0:4] + total[4:8], total[16:20] + total[20:24]], axis=0
    ) * gscale
    for q in range(4):
        out_local[pl.ds(q, 8, stride=4), :] = flat[:, 32 * q : 32 * (q + 1)]
    out_bias[...] = ((total[8:9] + total[9:10]) * gscale)[:, :32]
    for copy in copies[1:]:
        copy.start()
    for copy in copies:
        copy.wait()


def run(kernel, operands, outs, scratch, name, specs=None, out_specs=None):
    specs = specs or [VM] * len(operands)
    out_specs = out_specs or [VM] * len(outs)
    operands = [
        pltpu.with_memory_space_constraint(operand, pltpu.HBM) if spec is HBM else operand
        for operand, spec in zip(operands, specs)
    ]
    return pl.pallas_call(
        kernel,
        out_shape=[
            (pltpu.HBM if spec is HBM else jax.ShapeDtypeStruct)(*out)
            for out, spec in zip(outs, out_specs)
        ],
        in_specs=specs,
        out_specs=out_specs,
        scratch_shapes=scratch,
        compiler_params=pltpu.CompilerParams(vmem_limit_bytes=16 * 1024 * 1024),
        cost_estimate=pl.CostEstimate(
            flops=COST.get(name, 200_000_000), bytes_accessed=1 << 20, transcendentals=0
        ),
        name=name,
    )(*operands)


def exchange(values, *shape):
    blocks = values.reshape((128,) + shape)
    return lax.all_to_all(blocks, GX, 0, 0, tiled=True).reshape(values.shape)


def local(field, cotangent, spectral_weight, local_weight, bias):
    ytab, forward, inverse = (jnp.asarray(table) for table in tables())
    slab = ((512, 128), BF16)
    slab_wide = ((1280, 128), BF16)
    held = pltpu.VMEM((512, 128), F32)
    held_wide = pltpu.VMEM((1280, 128), F32)
    quarters = pltpu.VMEM((4, 4, C, N), BF16)

    send, bias_row, local_near = run(
        y_kernel,
        (field, ytab, bias.reshape(1, C), local_weight),
        [slab, ((1, C), F32), ((C, C), BF16)],
        [held, quarters, pltpu.VMEM((128, N), BF16), pltpu.SemaphoreType.DMA((7,))],
        "y_forward",
        [HBM] * 4,
    )
    recv = exchange(send, 4, 128)
    weight = lax.all_gather(spectral_weight, "core", axis=0, tiled=True)
    send, first = run(
        mix_kernel,
        (recv, weight, forward, inverse),
        [slab, ((KX, 128), BF16)],
        [held],
        "mix",
    )
    recv = exchange(send, 4, 128)
    send, delta = run(
        point_kernel,
        (recv, field, cotangent, local_near, bias_row, ytab),
        [slab_wide, ((4, 128, N), BF16)],
        [
            held,
            held_wide,
        ],
        "pointwise",
    )
    recv = exchange(send, 5, 2, 128)
    second, share = run(
        back_kernel,
        (recv, forward, first),
        [((2 * KX, 128), F32), ((2 * KX + 16, 128), BF16)],
        [held_wide],
        "x_forward",
    )
    shares = lax.all_gather(share, "core", axis=0, tiled=True)
    send, group = run(
        adjoint_kernel,
        (second, weight, inverse, shares),
        [slab, ((160, 128), BF16)],
        [held, pltpu.VMEM((256, 1024), BF16), pltpu.VMEM((256, 1024), BF16)],
        "adjoint",
    )
    recv = exchange(send, 4, 128)
    for pairs in ([[0, 1], [2, 3]], [[0, 3], [1, 2]]):
        group = lax.all_gather(group, "gz", axis=0, tiled=True, axis_index_groups=pairs)
    field_grad, spectral_grad, local_grad, bias_grad = run(
        final_kernel,
        (recv, delta, local_near, ytab, group),
        [((8, 2, C, N), BF16), ((64, 2048), BF16), ((C, C), F32), ((1, C), F32)],
        [
            held,
            pltpu.VMEM((8, 2, C, N), BF16),
            pltpu.VMEM((64, 2048), BF16),
            pltpu.VMEM((1024, 128), F32),
            pltpu.VMEM((C, C), F32),
            pltpu.VMEM((1, C), F32),
            pltpu.SemaphoreType.DMA((4,)),
        ],
        "final",
        None,
        [HBM] * 4,
    )
    return field_grad, spectral_grad, local_grad, bias_grad.reshape(C)


def solution(mesh):
    fine = Mesh(mesh.devices.reshape(8, 8, 2, 4), GX + ("gz",))
    cells = P(GX, "gz", None, None)
    return jax.shard_map(
        local,
        mesh=fine,
        in_specs=(cells, cells, P(GX, None), P(), P()),
        out_specs=(cells, P(GX, None), P(), P()),
        check_vma=False,
    )
```

```python
import jax
import jax.numpy as jnp
import ml_dtypes
import numpy as np
from jax import lax
from jax.experimental import pallas as pl
from jax.experimental.pallas import tpu as pltpu
from jax.sharding import Mesh
from jax.sharding import PartitionSpec as P

KX = 128
KY = 64
C = 32
N = 1024
F32 = jnp.float32
BF16 = jnp.bfloat16
GX = ("y", "z", "core")
VM = pl.BlockSpec(memory_space=pltpu.VMEM)
HBM = pl.BlockSpec(memory_space=pltpu.HBM)
COST = {"mix": 800_000_000}


def angles(freq, pos):
    product = (freq[:, None].astype(np.int64) * pos[None, :].astype(np.int64)) % N
    angle = product.astype(np.float32) * np.float32(2.0 * np.pi / N)
    return np.cos(angle).astype(np.float32), np.sin(angle).astype(np.float32)


def tables():
    ycos, ysin = angles(np.arange(KY), np.arange(N))
    ytab = np.concatenate([ycos, -ysin], axis=0).astype(ml_dtypes.bfloat16)
    ytab = (ytab.astype(np.float32) / 32.0).astype(ml_dtypes.bfloat16)
    j = np.arange(KX)
    freq = np.where(j < KX // 2, j, j - KX)
    r, h, d = np.meshgrid(np.arange(4), np.arange(2), np.arange(128), indexing="ij")
    xcos, xsin = angles(freq, (8 * d + 4 * h + r).reshape(-1))
    forward = np.concatenate([xcos, xsin], axis=0).astype(ml_dtypes.bfloat16)
    inverse = forward.reshape(2 * KX, 4, 256).transpose(2, 1, 0).reshape(256, 1024)
    return ytab, forward, np.ascontiguousarray(inverse)


def nt(a, b):
    return lax.dot_general(a, b, (((1,), (1,)), ((), ())), preferred_element_type=F32)


def nn(a, b):
    return jnp.dot(a, b, preferred_element_type=F32)


def block_of(shape):
    return (lax.broadcasted_iota(jnp.int32, shape, 1) >> 5) & 3


def fold(v):
    v = v + pltpu.roll(v, 64, 1)
    return v + pltpu.roll(v, 32, 1)


def spread(base):
    block = block_of(base.shape)
    return jnp.concatenate([jnp.where(block == r, base, 0.0) for r in range(4)], axis=0).astype(BF16)


def rounded(v):
    return v.astype(BF16).astype(F32)


def mode_weight():
    first = (lax.axis_index("y") + lax.axis_index("z")) == 0
    return jnp.where(first, 1.0, 2.0).astype(F32)


def x_forward(recv, table, held, stride):
    held[...] = recv[...].astype(F32)
    parts = [
        jnp.concatenate([held[pl.ds(2 * p + h, 128, stride=stride), :] for h in range(2)], axis=0)
        for p in range(2)
    ]
    out = nn(table[...], spread(jnp.concatenate(parts, axis=1)))
    real = out[:KX, :128] + out[KX:, 128:]
    imag = out[:KX, 128:] - out[KX:, :128]
    return fold(real) * (1.0 / 32.0), fold(imag) * (1.0 / 32.0)


def packed(real, imag):
    both = jnp.where((block_of(real.shape) & 1) == 0, real, imag)
    return jnp.where(block_of((64, 128)) < 2, both[:64], both[64:]).astype(BF16)


def x_inverse(real, imag, table, held, stride):
    base = jnp.concatenate(
        [jnp.concatenate([real, imag], axis=1), jnp.concatenate([-imag, real], axis=1)], axis=0
    )
    out = nn(table[...], spread(base)) * (1.0 / 32.0)
    for p in range(2):
        for h in range(2):
            held[pl.ds(2 * p + h, 128, stride=stride), :] = out[
                128 * h : 128 * (h + 1), 128 * p : 128 * (p + 1)
            ]


def y_kernel(field, ytab, bias, local, send, bias_row, local_near, held, rows, table, sems):
    copies = [pltpu.make_async_copy(ytab, table, sems.at[4])]
    for k in range(4):
        part = field.at[pl.ds(4 * (k % 2), 4), k // 2]
        copies.append(pltpu.make_async_copy(part, rows.at[k], sems.at[k]))
    copies.append(pltpu.make_async_copy(bias, bias_row, sems.at[5]))
    copies.append(pltpu.make_async_copy(local, local_near, sems.at[6]))
    for copy in copies:
        copy.start()
    for k in range(4):
        z, h = k // 2, k % 2
        if h == 0:
            for copy in copies[3 * z : 3 + 4 * z]:
                copy.wait()
        out = nt(table[...], rows[k].reshape(128, N))
        for p in range(2):
            held[pl.ds(4 * z + 2 * p + h, KY, stride=8), :] = out[KY * p : KY * (p + 1)]
    send[...] = held[...].astype(BF16)


def mix_kernel(recv, weight, forward, inverse, send, kept, held):
    real, imag = x_forward(recv, forward, held, 4)
    real = rounded(real)
    imag = rounded(imag)
    kept[...] = packed(real, imag)
    k = lax.broadcasted_iota(jnp.int32, (128, 1024), 0)
    lane = lax.broadcasted_iota(jnp.int32, (128, 1024), 1)
    expand = jnp.where((lane >> 5) == k, 1.0, 0.0).astype(BF16)
    wide = nn(jnp.concatenate([real, imag], axis=0).astype(BF16), expand)
    vre = jnp.zeros((KX, 128), F32)
    vim = jnp.zeros((KX, 128), F32)
    for t in range(8):
        wre = weight[:, 128 * t : 128 * (t + 1)].astype(F32)
        wim = weight[:, 1024 + 128 * t : 1024 + 128 * (t + 1)].astype(F32)
        ure = wide[:KX, 128 * t : 128 * (t + 1)]
        uim = wide[KX:, 128 * t : 128 * (t + 1)]
        vre = vre + (ure * wre - uim * wim)
        vim = vim + (ure * wim + uim * wre)
    factor = mode_weight()
    x_inverse(rounded(fold(vre) * factor), rounded(fold(vim) * factor), inverse, held, 4)
    send[...] = held[...].astype(BF16)


def repeats():
    row = lax.broadcasted_iota(jnp.int32, (128, C), 0)
    return jnp.where((row & 31) == lax.broadcasted_iota(jnp.int32, (128, C), 1), 1.0, 0.0)


def blocks(tall, picks):
    row = lax.broadcasted_iota(jnp.int32, (128, 128), 0)
    wide = nt(tall.astype(BF16), picks)
    return jnp.where((row >> 5) == block_of((128, 128)), wide, 0.0).astype(BF16)


def point_kernel(recv, field, cotangent, local, bias, ytab, send, delta, held, wide):
    held[...] = recv[...].astype(F32)
    same = repeats()
    bias4 = jnp.sum(same * bias[...], axis=1, keepdims=True)
    picks = same.astype(BF16)
    local4 = blocks(nt(picks, local[...]), picks)
    ones = jnp.ones((16, N), BF16)
    total = jnp.zeros((144, 128), F32)
    outs = []
    for k in range(4):
        z, h = k // 2, k % 2
        spectrum = jnp.concatenate(
            [held[pl.ds(4 * z + 2 * p + h, KY, stride=8), :] for p in range(2)], axis=0
        )
        left = jnp.concatenate([spectrum.T.astype(BF16), local4], axis=1)
        rows = field[4 * h : 4 * h + 4, z].reshape(128, N)
        cot = cotangent[4 * h : 4 * h + 4, z].reshape(128, N)
        for part in range(4):
            cols = slice(256 * part, 256 * (part + 1))
            right = jnp.concatenate([ytab[:, cols], rows[:, cols]], axis=0)
            pre = nn(left, right) + bias4
            sig = 0.5 * jnp.tanh(0.5 * pre) + 0.5
            slope = sig * (1.0 + pre * (1.0 - sig))
            delta[k, :, cols] = (cot[:, cols].astype(F32) * slope).astype(BF16)
    for k in range(4):
        z, h = k // 2, k % 2
        rows = field[4 * h : 4 * h + 4, z].reshape(128, N)
        out = nt(jnp.concatenate([ytab[...], rows, ones], axis=0), delta[k])
        outs.append((z, h, out[:128]))
        total = total + out[128:]
    bias_total = total[128:]
    block = block_of((32, 128))
    diag = jnp.zeros((32, 128), F32)
    for r in range(4):
        diag = diag + jnp.where(block == r, total[32 * r : 32 * (r + 1)], 0.0)
    held[0:32, :] = fold(diag)
    block = block_of((8, 128))
    flat = jnp.zeros((8, 128), F32)
    for q in range(4):
        flat = flat + jnp.where(block == q, held[pl.ds(q, 8, stride=4), :], 0.0)
    bias = fold(bias_total[0:8])[0:1]
    bias_1 = rounded(bias)
    bias_2 = rounded(bias - bias_1)
    bias_3 = bias - bias_1 - bias_2
    block = block_of((1, 128))
    pieces = jnp.where(
        block == 0, bias_1, jnp.where(block == 1, bias_2, jnp.where(block == 2, bias_3, 0.0))
    )
    for z, h, out in outs:
        for p in range(2):
            wide[pl.ds(10 * z + 2 * p + h, KY, stride=20), :] = out[KY * p : KY * (p + 1)]
    for z in range(2):
        lines = [flat[4 * z + k : 4 * z + k + 1] for k in range(4)]
        lines = lines + [pieces, jnp.zeros((1, 128), F32)]
        for k, line in enumerate(lines):
            wide[pl.ds(10 * z + 4 + k, KY, stride=20), :] = jnp.broadcast_to(line, (KY, 128))
    send[...] = wide[...].astype(BF16)


def back_kernel(recv, forward, first, kept, share, held):
    real, imag = x_forward(recv, forward, held, 10)
    factor = mode_weight()
    real = rounded(real * factor)
    imag = rounded(imag * factor)
    kept[:KX] = real
    kept[KX:] = imag
    share[:64] = first[...]
    share[64:128] = packed(real, imag)
    lines = [
        jnp.sum(held[pl.ds(4 + k, 128, stride=10), :], axis=0, keepdims=True) for k in range(5)
    ]
    total = jnp.concatenate(lines[:4], axis=0)
    bias = fold(lines[4])
    share[128:] = jnp.concatenate(
        [
            rounded(total),
            total - rounded(total),
            rounded(bias),
            bias - rounded(bias),
            jnp.zeros((6, 128), F32),
        ],
        axis=0,
    ).astype(BF16)


def adjoint_kernel(kept, weight, inverse, share, send, group, held, high, low):
    dre = kept[:KX]
    dim = kept[KX:]
    for t in range(8):
        cols = slice(128 * t, 128 * (t + 1))
        wre = weight[:, cols].astype(F32)
        wim = weight[:, 1024 + 128 * t : 1024 + 128 * (t + 1)].astype(F32)
        for k, term in ((0, dre * wre + dim * wim), (1, dim * wre - dre * wim)):
            top = term.astype(BF16)
            high[KX * k : KX * (k + 1), cols] = top
            low[KX * k : KX * (k + 1), cols] = (term - top.astype(F32)).astype(BF16)
    k = lax.broadcasted_iota(jnp.int32, (1024, 128), 0)
    lane = lax.broadcasted_iota(jnp.int32, (1024, 128), 1)
    gather = jnp.where((k >> 5) == (lane & 31), 1.0, 0.0).astype(BF16)
    back = rounded(nn(high[...], gather) + nn(low[...], gather))
    x_inverse(back[:KX], back[KX:], inverse, held, 4)
    send[...] = held[...].astype(BF16)
    group[...] = share[...]


def final_kernel(
    recv, delta, local, ytab, groups, field_grad, spectral_grad, local_grad, bias_grad,
    held, rows, out, tiles, out_local, out_bias, sems,
):
    held[...] = recv[...].astype(F32)
    picks = repeats().astype(BF16)
    local4 = blocks(nn(picks, local[...]), picks)
    copies = [
        pltpu.make_async_copy(rows, field_grad, sems.at[0]),
        pltpu.make_async_copy(out, spectral_grad, sems.at[1]),
        pltpu.make_async_copy(out_local, local_grad, sems.at[2]),
        pltpu.make_async_copy(out_bias, bias_grad, sems.at[3]),
    ]
    for k in range(4):
        z, h = k // 2, k % 2
        spectrum = jnp.concatenate(
            [held[pl.ds(4 * z + 2 * p + h, KY, stride=8), :] for p in range(2)], axis=0
        )
        left = jnp.concatenate([spectrum.T.astype(BF16), local4], axis=1)
        for part in range(4):
            cols = slice(256 * part, 256 * (part + 1))
            right = jnp.concatenate([ytab[:, cols], delta[k, :, cols]], axis=0)
            rows[4 * h : 4 * h + 4, z, :, cols] = nn(left, right).astype(BF16).reshape(4, 32, 256)
    copies[0].start()
    lane = lax.broadcasted_iota(jnp.int32, (128, 1024), 1)
    k = lax.broadcasted_iota(jnp.int32, (128, 1024), 0)
    expand = jnp.where((lane >> 5) == k, 1.0, 0.0).astype(BF16)
    second_half = lax.axis_index("core") == 1

    def own(at):
        both = groups[at : at + 64].astype(F32)
        return jnp.where(second_half, pltpu.roll(both, 64, 1), both)

    first = jnp.concatenate([own(144 * g) for g in range(8)], axis=0)
    compact = jnp.concatenate([first, pltpu.roll(first, 96, 1)], axis=0).astype(BF16)
    block = block_of((64, 128))
    for g in range(8):
        second = own(144 * g + 64)
        for part in range(2):
            tiles[64 * (8 * part + g) : 64 * (8 * part + g + 1)] = fold(
                jnp.where(block == part, second, 0.0)
            )
    for pair in range(4):
        wide = nn(compact, expand[:, 256 * pair : 256 * (pair + 1)])
        for half in range(2):
            t = 2 * pair + half
            cols = slice(128 * half, 128 * (half + 1))
            real = jnp.zeros((64, 128), F32)
            imag = jnp.zeros((64, 128), F32)
            for g in range(8):
                ure = wide[64 * g : 64 * (g + 1), cols]
                uim = wide[512 + 64 * g : 512 + 64 * (g + 1), cols]
                dre = tiles[64 * g : 64 * (g + 1)]
                dim = tiles[512 + 64 * g : 512 + 64 * (g + 1)]
                real = real + (ure * dre + uim * dim)
                imag = imag + (ure * dim - uim * dre)
            out[:, 128 * t : 128 * (t + 1)] = real.astype(BF16)
            out[:, 1024 + 128 * t : 1024 + 128 * (t + 1)] = imag.astype(BF16)
    gscale = float((N * N * 8) ** -0.5)
    halves = []
    for c in range(2):
        total = jnp.zeros((16, 128), F32)
        for g in range(4):
            at = 144 * (4 * c + g) + 128
            total = total + groups[at : at + 16].astype(F32)
        halves.append(total)
    flat = jnp.concatenate([total[0:4] + total[4:8] for total in halves], axis=0) * gscale
    total = halves[0]
    for q in range(4):
        out_local[pl.ds(q, 8, stride=4), :] = flat[:, 32 * q : 32 * (q + 1)]
    out_bias[...] = ((total[8:9] + total[9:10]) * gscale)[:, :32]
    for copy in copies[1:]:
        copy.start()
    for copy in copies:
        copy.wait()


def run(kernel, operands, outs, scratch, name, specs=None, out_specs=None):
    specs = specs or [VM] * len(operands)
    out_specs = out_specs or [VM] * len(outs)
    operands = [
        pltpu.with_memory_space_constraint(operand, pltpu.HBM) if spec is HBM else operand
        for operand, spec in zip(operands, specs)
    ]
    return pl.pallas_call(
        kernel,
        out_shape=[
            (pltpu.HBM if spec is HBM else jax.ShapeDtypeStruct)(*out)
            for out, spec in zip(outs, out_specs)
        ],
        in_specs=specs,
        out_specs=out_specs,
        scratch_shapes=scratch,
        compiler_params=pltpu.CompilerParams(vmem_limit_bytes=16 * 1024 * 1024),
        cost_estimate=pl.CostEstimate(
            flops=COST.get(name, 200_000_000), bytes_accessed=1 << 20, transcendentals=0
        ),
        name=name,
    )(*operands)


def exchange(values, *shape):
    blocks = values.reshape((128,) + shape)
    return lax.all_to_all(blocks, GX, 0, 0, tiled=True).reshape(values.shape)


def local(field, cotangent, spectral_weight, local_weight, bias):
    ytab, forward, inverse = (jnp.asarray(table) for table in tables())
    slab = ((512, 128), BF16)
    slab_wide = ((1280, 128), BF16)
    held = pltpu.VMEM((512, 128), F32)
    held_wide = pltpu.VMEM((1280, 128), F32)
    quarters = pltpu.VMEM((4, 4, C, N), BF16)

    send, bias_row, local_near = run(
        y_kernel,
        (field, ytab, bias.reshape(1, C), local_weight),
        [slab, ((1, C), F32), ((C, C), BF16)],
        [held, quarters, pltpu.VMEM((128, N), BF16), pltpu.SemaphoreType.DMA((7,))],
        "y_forward",
        [HBM] * 4,
    )
    recv = exchange(send, 4, 128)
    weight = lax.all_gather(spectral_weight, "core", axis=0, tiled=True)
    send, first = run(
        mix_kernel,
        (recv, weight, forward, inverse),
        [slab, ((64, 128), BF16)],
        [held],
        "mix",
    )
    recv = exchange(send, 4, 128)
    send, delta = run(
        point_kernel,
        (recv, field, cotangent, local_near, bias_row, ytab),
        [slab_wide, ((4, 128, N), BF16)],
        [
            held,
            held_wide,
        ],
        "pointwise",
    )
    recv = exchange(send, 5, 2, 128)
    second, share = run(
        back_kernel,
        (recv, forward, first),
        [((2 * KX, 128), F32), ((144, 128), BF16)],
        [held_wide],
        "x_forward",
    )
    send, group = run(
        adjoint_kernel,
        (second, weight, inverse, share),
        [slab, ((144, 128), BF16)],
        [held, pltpu.VMEM((256, 1024), BF16), pltpu.VMEM((256, 1024), BF16)],
        "adjoint",
    )
    recv = exchange(send, 4, 128)
    for pairs in ([[0, 1], [2, 3]], [[0, 3], [1, 2]]):
        group = lax.all_gather(group, "gz", axis=0, tiled=True, axis_index_groups=pairs)
    group = lax.all_gather(group, "core", axis=0, tiled=True)
    field_grad, spectral_grad, local_grad, bias_grad = run(
        final_kernel,
        (recv, delta, local_near, ytab, group),
        [((8, 2, C, N), BF16), ((64, 2048), BF16), ((C, C), F32), ((1, C), F32)],
        [
            held,
            pltpu.VMEM((8, 2, C, N), BF16),
            pltpu.VMEM((64, 2048), BF16),
            pltpu.VMEM((1024, 128), F32),
            pltpu.VMEM((C, C), F32),
            pltpu.VMEM((1, C), F32),
            pltpu.SemaphoreType.DMA((4,)),
        ],
        "final",
        None,
        [HBM] * 4,
    )
    return field_grad, spectral_grad, local_grad, bias_grad.reshape(C)


def solution(mesh):
    fine = Mesh(mesh.devices.reshape(8, 8, 2, 4), GX + ("gz",))
    cells = P(GX, "gz", None, None)
    return jax.shard_map(
        local,
        mesh=fine,
        in_specs=(cells, cells, P(GX, None), P(), P()),
        out_specs=(cells, P(GX, None), P(), P()),
        check_vma=False,
    )
```

```python
import jax
import jax.numpy as jnp
import ml_dtypes
import numpy as np
from jax import lax
from jax.experimental import pallas as pl
from jax.experimental.pallas import tpu as pltpu
from jax.sharding import Mesh
from jax.sharding import PartitionSpec as P

KX = 128
KY = 64
C = 32
N = 1024
F32 = jnp.float32
BF16 = jnp.bfloat16
GX = ("y", "z", "core")
VM = pl.BlockSpec(memory_space=pltpu.VMEM)
HBM = pl.BlockSpec(memory_space=pltpu.HBM)
COST = {"mix": 800_000_000}


def angles(freq, pos):
    product = (freq[:, None].astype(np.int64) * pos[None, :].astype(np.int64)) % N
    angle = product.astype(np.float32) * np.float32(2.0 * np.pi / N)
    return np.cos(angle).astype(np.float32), np.sin(angle).astype(np.float32)


def tables():
    ycos, ysin = angles(np.arange(KY), np.arange(N))
    ytab = np.concatenate([ycos, -ysin], axis=0).astype(ml_dtypes.bfloat16)
    ytab = (ytab.astype(np.float32) / 32.0).astype(ml_dtypes.bfloat16)
    j = np.arange(KX)
    freq = np.where(j < KX // 2, j, j - KX)
    r, h, d = np.meshgrid(np.arange(4), np.arange(2), np.arange(128), indexing="ij")
    xcos, xsin = angles(freq, (8 * d + 4 * h + r).reshape(-1))
    forward = np.concatenate([xcos, xsin], axis=0).astype(ml_dtypes.bfloat16)
    inverse = forward.reshape(2 * KX, 4, 256).transpose(2, 1, 0).reshape(256, 1024)
    return ytab, forward, np.ascontiguousarray(inverse)


def nt(a, b):
    return lax.dot_general(a, b, (((1,), (1,)), ((), ())), preferred_element_type=F32)


def nn(a, b):
    return jnp.dot(a, b, preferred_element_type=F32)


def block_of(shape):
    return (lax.broadcasted_iota(jnp.int32, shape, 1) >> 5) & 3


def fold(v):
    v = v + pltpu.roll(v, 64, 1)
    return v + pltpu.roll(v, 32, 1)


def spread(base):
    block = block_of(base.shape)
    return jnp.concatenate([jnp.where(block == r, base, 0.0) for r in range(4)], axis=0).astype(BF16)


def rounded(v):
    return v.astype(BF16).astype(F32)


def mode_weight():
    first = (lax.axis_index("y") + lax.axis_index("z")) == 0
    return jnp.where(first, 1.0, 2.0).astype(F32)


def x_forward(recv, table, held, stride):
    held[...] = recv[...].astype(F32)
    parts = [
        jnp.concatenate([held[pl.ds(2 * p + h, 128, stride=stride), :] for h in range(2)], axis=0)
        for p in range(2)
    ]
    out = nn(table[...], spread(jnp.concatenate(parts, axis=1)))
    real = out[:KX, :128] + out[KX:, 128:]
    imag = out[:KX, 128:] - out[KX:, :128]
    return fold(real) * (1.0 / 32.0), fold(imag) * (1.0 / 32.0)


def packed(real, imag):
    both = jnp.where((block_of(real.shape) & 1) == 0, real, imag)
    return jnp.where(block_of((64, 128)) < 2, both[:64], both[64:]).astype(BF16)


def x_inverse(real, imag, table, held, stride):
    base = jnp.concatenate(
        [jnp.concatenate([real, imag], axis=1), jnp.concatenate([-imag, real], axis=1)], axis=0
    )
    out = nn(table[...], spread(base)) * (1.0 / 32.0)
    for p in range(2):
        for h in range(2):
            held[pl.ds(2 * p + h, 128, stride=stride), :] = out[
                128 * h : 128 * (h + 1), 128 * p : 128 * (p + 1)
            ]


def y_kernel(field, ytab, bias, local, send, bias_row, local_near, held, rows, table, sems):
    copies = [pltpu.make_async_copy(ytab, table, sems.at[4])]
    for k in range(4):
        part = field.at[pl.ds(4 * (k % 2), 4), k // 2]
        copies.append(pltpu.make_async_copy(part, rows.at[k], sems.at[k]))
    copies.append(pltpu.make_async_copy(bias, bias_row, sems.at[5]))
    copies.append(pltpu.make_async_copy(local, local_near, sems.at[6]))
    for copy in copies:
        copy.start()
    for k in range(4):
        z, h = k // 2, k % 2
        if h == 0:
            for copy in copies[3 * z : 3 + 4 * z]:
                copy.wait()
        out = nt(table[...], rows[k].reshape(128, N))
        for p in range(2):
            held[pl.ds(4 * z + 2 * p + h, KY, stride=8), :] = out[KY * p : KY * (p + 1)]
    send[...] = held[...].astype(BF16)


def mix_kernel(recv, weight, forward, inverse, send, kept, held):
    real, imag = x_forward(recv, forward, held, 4)
    real = rounded(real)
    imag = rounded(imag)
    kept[...] = packed(real, imag)
    k = lax.broadcasted_iota(jnp.int32, (128, 1024), 0)
    lane = lax.broadcasted_iota(jnp.int32, (128, 1024), 1)
    expand = jnp.where((lane >> 5) == k, 1.0, 0.0).astype(BF16)
    wide = nn(jnp.concatenate([real, imag], axis=0).astype(BF16), expand)
    vre = jnp.zeros((KX, 128), F32)
    vim = jnp.zeros((KX, 128), F32)
    for t in range(8):
        wre = weight[:, 128 * t : 128 * (t + 1)].astype(F32)
        wim = weight[:, 1024 + 128 * t : 1024 + 128 * (t + 1)].astype(F32)
        ure = wide[:KX, 128 * t : 128 * (t + 1)]
        uim = wide[KX:, 128 * t : 128 * (t + 1)]
        vre = vre + (ure * wre - uim * wim)
        vim = vim + (ure * wim + uim * wre)
    factor = mode_weight()
    x_inverse(rounded(fold(vre) * factor), rounded(fold(vim) * factor), inverse, held, 4)
    send[...] = held[...].astype(BF16)


def repeats():
    row = lax.broadcasted_iota(jnp.int32, (128, C), 0)
    return jnp.where((row & 31) == lax.broadcasted_iota(jnp.int32, (128, C), 1), 1.0, 0.0)


def blocks(tall, picks):
    row = lax.broadcasted_iota(jnp.int32, (128, 128), 0)
    wide = nt(tall.astype(BF16), picks)
    return jnp.where((row >> 5) == block_of((128, 128)), wide, 0.0).astype(BF16)


def point_kernel(recv, field, cotangent, local, bias, ytab, send, delta, held, wide):
    held[...] = recv[...].astype(F32)
    same = repeats()
    bias4 = jnp.sum(same * bias[...], axis=1, keepdims=True)
    picks = same.astype(BF16)
    local4 = blocks(nt(picks, local[...]), picks)
    ones = jnp.ones((16, N), BF16)
    total = jnp.zeros((144, 128), F32)
    outs = []
    for k in range(4):
        z, h = k // 2, k % 2
        spectrum = jnp.concatenate(
            [held[pl.ds(4 * z + 2 * p + h, KY, stride=8), :] for p in range(2)], axis=0
        )
        left = jnp.concatenate([spectrum.T.astype(BF16), local4], axis=1)
        rows = field[4 * h : 4 * h + 4, z].reshape(128, N)
        cot = cotangent[4 * h : 4 * h + 4, z].reshape(128, N)
        for part in range(4):
            cols = slice(256 * part, 256 * (part + 1))
            right = jnp.concatenate([ytab[:, cols], rows[:, cols]], axis=0)
            pre = nn(left, right) + bias4
            sig = 0.5 * jnp.tanh(0.5 * pre) + 0.5
            slope = sig * (1.0 + pre * (1.0 - sig))
            delta[k, :, cols] = (cot[:, cols].astype(F32) * slope).astype(BF16)
    for k in range(4):
        z, h = k // 2, k % 2
        rows = field[4 * h : 4 * h + 4, z].reshape(128, N)
        out = nt(jnp.concatenate([ytab[...], rows, ones], axis=0), delta[k])
        outs.append((z, h, out[:128]))
        total = total + out[128:]
    bias_total = total[128:]
    block = block_of((32, 128))
    diag = jnp.zeros((32, 128), F32)
    for r in range(4):
        diag = diag + jnp.where(block == r, total[32 * r : 32 * (r + 1)], 0.0)
    held[0:32, :] = fold(diag)
    block = block_of((8, 128))
    flat = jnp.zeros((8, 128), F32)
    for q in range(4):
        flat = flat + jnp.where(block == q, held[pl.ds(q, 8, stride=4), :], 0.0)
    bias = fold(bias_total[0:8])[0:1]
    bias_1 = rounded(bias)
    bias_2 = rounded(bias - bias_1)
    bias_3 = bias - bias_1 - bias_2
    block = block_of((1, 128))
    pieces = jnp.where(
        block == 0, bias_1, jnp.where(block == 1, bias_2, jnp.where(block == 2, bias_3, 0.0))
    )
    for z, h, out in outs:
        for p in range(2):
            wide[pl.ds(10 * z + 2 * p + h, KY, stride=20), :] = out[KY * p : KY * (p + 1)]
    for z in range(2):
        lines = [flat[4 * z + k : 4 * z + k + 1] for k in range(4)]
        lines = lines + [pieces, jnp.zeros((1, 128), F32)]
        for k, line in enumerate(lines):
            wide[pl.ds(10 * z + 4 + k, KY, stride=20), :] = jnp.broadcast_to(line, (KY, 128))
    send[...] = wide[...].astype(BF16)


def back_kernel(recv, forward, first, kept, share, held):
    real, imag = x_forward(recv, forward, held, 10)
    factor = mode_weight()
    real = rounded(real * factor)
    imag = rounded(imag * factor)
    kept[:KX] = real
    kept[KX:] = imag
    share[:64] = first[...]
    share[64:128] = packed(real, imag)
    lines = [
        jnp.sum(held[pl.ds(4 + k, 128, stride=10), :], axis=0, keepdims=True) for k in range(5)
    ]
    total = jnp.concatenate(lines[:4], axis=0)
    bias = fold(lines[4])
    share[128:] = jnp.concatenate(
        [
            rounded(total),
            total - rounded(total),
            rounded(bias),
            bias - rounded(bias),
            jnp.zeros((6, 128), F32),
        ],
        axis=0,
    ).astype(BF16)


def adjoint_kernel(kept, weight, inverse, share, send, group, held, high, low):
    dre = kept[:KX]
    dim = kept[KX:]
    for t in range(8):
        cols = slice(128 * t, 128 * (t + 1))
        wre = weight[:, cols].astype(F32)
        wim = weight[:, 1024 + 128 * t : 1024 + 128 * (t + 1)].astype(F32)
        for k, term in ((0, dre * wre + dim * wim), (1, dim * wre - dre * wim)):
            top = term.astype(BF16)
            high[KX * k : KX * (k + 1), cols] = top
            low[KX * k : KX * (k + 1), cols] = (term - top.astype(F32)).astype(BF16)
    k = lax.broadcasted_iota(jnp.int32, (1024, 128), 0)
    lane = lax.broadcasted_iota(jnp.int32, (1024, 128), 1)
    gather = jnp.where((k >> 5) == (lane & 31), 1.0, 0.0).astype(BF16)
    back = rounded(nn(high[...], gather) + nn(low[...], gather))
    x_inverse(back[:KX], back[KX:], inverse, held, 4)
    send[...] = held[...].astype(BF16)
    group[...] = share[...]


def final_kernel(
    recv, delta, local, ytab, groups, field_grad, spectral_grad, local_grad, bias_grad,
    held, rows, out, tiles, out_local, out_bias, sems,
):
    held[...] = recv[...].astype(F32)
    picks = repeats().astype(BF16)
    local4 = blocks(nn(picks, local[...]), picks)
    copies = [
        pltpu.make_async_copy(rows, field_grad, sems.at[0]),
        pltpu.make_async_copy(out, spectral_grad, sems.at[1]),
        pltpu.make_async_copy(out_local, local_grad, sems.at[2]),
        pltpu.make_async_copy(out_bias, bias_grad, sems.at[3]),
    ]
    for k in range(4):
        z, h = k // 2, k % 2
        spectrum = jnp.concatenate(
            [held[pl.ds(4 * z + 2 * p + h, KY, stride=8), :] for p in range(2)], axis=0
        )
        left = jnp.concatenate([spectrum.T.astype(BF16), local4], axis=1)
        for part in range(4):
            cols = slice(256 * part, 256 * (part + 1))
            right = jnp.concatenate([ytab[:, cols], delta[k, :, cols]], axis=0)
            rows[4 * h : 4 * h + 4, z, :, cols] = nn(left, right).astype(BF16).reshape(4, 32, 256)
    copies[0].start()
    lane = lax.broadcasted_iota(jnp.int32, (128, 1024), 1)
    k = lax.broadcasted_iota(jnp.int32, (128, 1024), 0)
    start = 64 * lax.axis_index("core")
    expands = [
        jnp.where((lane >> 5) + (start + 32 * part) == k, 1.0, 0.0).astype(BF16)
        for part in range(2)
    ]
    compact = jnp.concatenate([groups[144 * g : 144 * g + 64] for g in range(8)], axis=0)
    block = block_of((64, 128)) - 2 * lax.axis_index("core")
    for g in range(8):
        second = groups[144 * g + 64 : 144 * g + 128].astype(F32)
        for part in range(2):
            tiles[64 * (8 * part + g) : 64 * (8 * part + g + 1)] = fold(
                jnp.where(block == part, second, 0.0)
            )
    for pair in range(4):
        wide = [nn(compact, expand[:, 256 * pair : 256 * (pair + 1)]) for expand in expands]
        for half in range(2):
            t = 2 * pair + half
            cols = slice(128 * half, 128 * (half + 1))
            real = jnp.zeros((64, 128), F32)
            imag = jnp.zeros((64, 128), F32)
            for g in range(8):
                ure = wide[0][64 * g : 64 * (g + 1), cols]
                uim = wide[1][64 * g : 64 * (g + 1), cols]
                dre = tiles[64 * g : 64 * (g + 1)]
                dim = tiles[512 + 64 * g : 512 + 64 * (g + 1)]
                real = real + (ure * dre + uim * dim)
                imag = imag + (ure * dim - uim * dre)
            out[:, 128 * t : 128 * (t + 1)] = real.astype(BF16)
            out[:, 1024 + 128 * t : 1024 + 128 * (t + 1)] = imag.astype(BF16)
    gscale = float((N * N * 8) ** -0.5)
    halves = []
    for c in range(2):
        total = jnp.zeros((16, 128), F32)
        for g in range(4):
            at = 144 * (4 * c + g) + 128
            total = total + groups[at : at + 16].astype(F32)
        halves.append(total)
    flat = jnp.concatenate([total[0:4] + total[4:8] for total in halves], axis=0) * gscale
    total = halves[0]
    for q in range(4):
        out_local[pl.ds(q, 8, stride=4), :] = flat[:, 32 * q : 32 * (q + 1)]
    out_bias[...] = ((total[8:9] + total[9:10]) * gscale)[:, :32]
    for copy in copies[1:]:
        copy.start()
    for copy in copies:
        copy.wait()


def run(kernel, operands, outs, scratch, name, specs=None, out_specs=None):
    specs = specs or [VM] * len(operands)
    out_specs = out_specs or [VM] * len(outs)
    operands = [
        pltpu.with_memory_space_constraint(operand, pltpu.HBM) if spec is HBM else operand
        for operand, spec in zip(operands, specs)
    ]
    return pl.pallas_call(
        kernel,
        out_shape=[
            (pltpu.HBM if spec is HBM else jax.ShapeDtypeStruct)(*out)
            for out, spec in zip(outs, out_specs)
        ],
        in_specs=specs,
        out_specs=out_specs,
        scratch_shapes=scratch,
        compiler_params=pltpu.CompilerParams(vmem_limit_bytes=16 * 1024 * 1024),
        cost_estimate=pl.CostEstimate(
            flops=COST.get(name, 200_000_000), bytes_accessed=1 << 20, transcendentals=0
        ),
        name=name,
    )(*operands)


def exchange(values, *shape):
    blocks = values.reshape((128,) + shape)
    return lax.all_to_all(blocks, GX, 0, 0, tiled=True).reshape(values.shape)


def local(field, cotangent, spectral_weight, local_weight, bias):
    ytab, forward, inverse = (jnp.asarray(table) for table in tables())
    slab = ((512, 128), BF16)
    slab_wide = ((1280, 128), BF16)
    held = pltpu.VMEM((512, 128), F32)
    held_wide = pltpu.VMEM((1280, 128), F32)
    quarters = pltpu.VMEM((4, 4, C, N), BF16)

    send, bias_row, local_near = run(
        y_kernel,
        (field, ytab, bias.reshape(1, C), local_weight),
        [slab, ((1, C), F32), ((C, C), BF16)],
        [held, quarters, pltpu.VMEM((128, N), BF16), pltpu.SemaphoreType.DMA((7,))],
        "y_forward",
        [HBM] * 4,
    )
    recv = exchange(send, 4, 128)
    weight = lax.all_gather(spectral_weight, "core", axis=0, tiled=True)
    send, first = run(
        mix_kernel,
        (recv, weight, forward, inverse),
        [slab, ((64, 128), BF16)],
        [held],
        "mix",
    )
    recv = exchange(send, 4, 128)
    send, delta = run(
        point_kernel,
        (recv, field, cotangent, local_near, bias_row, ytab),
        [slab_wide, ((4, 128, N), BF16)],
        [
            held,
            held_wide,
        ],
        "pointwise",
    )
    recv = exchange(send, 5, 2, 128)
    second, share = run(
        back_kernel,
        (recv, forward, first),
        [((2 * KX, 128), F32), ((144, 128), BF16)],
        [held_wide],
        "x_forward",
    )
    send, group = run(
        adjoint_kernel,
        (second, weight, inverse, share),
        [slab, ((144, 128), BF16)],
        [held, pltpu.VMEM((256, 1024), BF16), pltpu.VMEM((256, 1024), BF16)],
        "adjoint",
    )
    recv = exchange(send, 4, 128)
    for pairs in ([[0, 1], [2, 3]], [[0, 3], [1, 2]]):
        group = lax.all_gather(group, "gz", axis=0, tiled=True, axis_index_groups=pairs)
    group = lax.all_gather(group, "core", axis=0, tiled=True)
    field_grad, spectral_grad, local_grad, bias_grad = run(
        final_kernel,
        (recv, delta, local_near, ytab, group),
        [((8, 2, C, N), BF16), ((64, 2048), BF16), ((C, C), F32), ((1, C), F32)],
        [
            held,
            pltpu.VMEM((8, 2, C, N), BF16),
            pltpu.VMEM((64, 2048), BF16),
            pltpu.VMEM((1024, 128), F32),
            pltpu.VMEM((C, C), F32),
            pltpu.VMEM((1, C), F32),
            pltpu.SemaphoreType.DMA((4,)),
        ],
        "final",
        None,
        [HBM] * 4,
    )
    return field_grad, spectral_grad, local_grad, bias_grad.reshape(C)


def solution(mesh):
    fine = Mesh(mesh.devices.reshape(8, 8, 2, 4), GX + ("gz",))
    cells = P(GX, "gz", None, None)
    return jax.shard_map(
        local,
        mesh=fine,
        in_specs=(cells, cells, P(GX, None), P(), P()),
        out_specs=(cells, P(GX, None), P(), P()),
        check_vma=False,
    )
```

```python
import jax
import jax.numpy as jnp
import ml_dtypes
import numpy as np
from jax import lax
from jax.experimental import pallas as pl
from jax.experimental.pallas import tpu as pltpu
from jax.sharding import Mesh
from jax.sharding import PartitionSpec as P

KX = 128
KY = 64
C = 32
N = 1024
F32 = jnp.float32
BF16 = jnp.bfloat16
GX = ("y", "z", "core")
VM = pl.BlockSpec(memory_space=pltpu.VMEM)
HBM = pl.BlockSpec(memory_space=pltpu.HBM)
COST = {"mix": 800_000_000}


def angles(freq, pos):
    product = (freq[:, None].astype(np.int64) * pos[None, :].astype(np.int64)) % N
    angle = product.astype(np.float32) * np.float32(2.0 * np.pi / N)
    return np.cos(angle).astype(np.float32), np.sin(angle).astype(np.float32)


def tables():
    ycos, ysin = angles(np.arange(KY), np.arange(N))
    ytab = np.concatenate([ycos, -ysin], axis=0).astype(ml_dtypes.bfloat16)
    ytab = (ytab.astype(np.float32) / 32.0).astype(ml_dtypes.bfloat16)
    j = np.arange(KX)
    freq = np.where(j < KX // 2, j, j - KX)
    r, h, d = np.meshgrid(np.arange(4), np.arange(2), np.arange(128), indexing="ij")
    xcos, xsin = angles(freq, (8 * d + 4 * h + r).reshape(-1))
    forward = np.concatenate([xcos, xsin], axis=0).astype(ml_dtypes.bfloat16)
    inverse = forward.reshape(2 * KX, 4, 256).transpose(2, 1, 0).reshape(256, 1024)
    return ytab, forward, np.ascontiguousarray(inverse)


def nt(a, b):
    return lax.dot_general(a, b, (((1,), (1,)), ((), ())), preferred_element_type=F32)


def nn(a, b):
    return jnp.dot(a, b, preferred_element_type=F32)


def block_of(shape):
    return (lax.broadcasted_iota(jnp.int32, shape, 1) >> 5) & 3


def fold(v):
    v = v + pltpu.roll(v, 64, 1)
    return v + pltpu.roll(v, 32, 1)


def spread(base):
    block = block_of(base.shape)
    return jnp.concatenate([jnp.where(block == r, base, 0.0) for r in range(4)], axis=0).astype(BF16)


def rounded(v):
    return v.astype(BF16).astype(F32)


def mode_weight():
    first = (lax.axis_index("y") + lax.axis_index("z")) == 0
    return jnp.where(first, 1.0, 2.0).astype(F32)


def x_forward(recv, table, held, stride):
    held[...] = recv[...].astype(F32)
    parts = [
        jnp.concatenate([held[pl.ds(2 * p + h, 128, stride=stride), :] for h in range(2)], axis=0)
        for p in range(2)
    ]
    out = nn(table[...], spread(jnp.concatenate(parts, axis=1)))
    real = out[:KX, :128] + out[KX:, 128:]
    imag = out[:KX, 128:] - out[KX:, :128]
    return fold(real) * (1.0 / 32.0), fold(imag) * (1.0 / 32.0)


def packed(real, imag):
    both = jnp.where((block_of(real.shape) & 1) == 0, real, imag)
    return jnp.where(block_of((64, 128)) < 2, both[:64], both[64:]).astype(BF16)


def x_inverse(real, imag, table, held, stride):
    base = jnp.concatenate(
        [jnp.concatenate([real, imag], axis=1), jnp.concatenate([-imag, real], axis=1)], axis=0
    )
    out = nn(table[...], spread(base)) * (1.0 / 32.0)
    for p in range(2):
        for h in range(2):
            held[pl.ds(2 * p + h, 128, stride=stride), :] = out[
                128 * h : 128 * (h + 1), 128 * p : 128 * (p + 1)
            ]


def y_kernel(field, ytab, bias, local, send, bias_row, local_near, held, rows, table, sems):
    copies = [pltpu.make_async_copy(ytab, table, sems.at[4])]
    for k in range(4):
        part = field.at[pl.ds(4 * (k % 2), 4), k // 2]
        copies.append(pltpu.make_async_copy(part, rows.at[k], sems.at[k]))
    copies.append(pltpu.make_async_copy(bias, bias_row, sems.at[5]))
    copies.append(pltpu.make_async_copy(local, local_near, sems.at[6]))
    for copy in copies:
        copy.start()
    for k in range(4):
        z, h = k // 2, k % 2
        if h == 0:
            for copy in copies[3 * z : 3 + 4 * z]:
                copy.wait()
        out = nt(table[...], rows[k].reshape(128, N))
        for p in range(2):
            held[pl.ds(4 * z + 2 * p + h, KY, stride=8), :] = out[KY * p : KY * (p + 1)]
    send[...] = held[...].astype(BF16)


def mix_kernel(recv, weight, forward, inverse, send, kept, held):
    real, imag = x_forward(recv, forward, held, 4)
    real = rounded(real)
    imag = rounded(imag)
    kept[...] = packed(real, imag)
    k = lax.broadcasted_iota(jnp.int32, (128, 1024), 0)
    lane = lax.broadcasted_iota(jnp.int32, (128, 1024), 1)
    expand = jnp.where((lane >> 5) == k, 1.0, 0.0).astype(BF16)
    wide = nn(jnp.concatenate([real, imag], axis=0).astype(BF16), expand)
    vre = jnp.zeros((KX, 128), F32)
    vim = jnp.zeros((KX, 128), F32)
    for t in range(8):
        wre = weight[:, 128 * t : 128 * (t + 1)].astype(F32)
        wim = weight[:, 1024 + 128 * t : 1024 + 128 * (t + 1)].astype(F32)
        ure = wide[:KX, 128 * t : 128 * (t + 1)]
        uim = wide[KX:, 128 * t : 128 * (t + 1)]
        vre = vre + (ure * wre - uim * wim)
        vim = vim + (ure * wim + uim * wre)
    factor = mode_weight()
    x_inverse(rounded(fold(vre) * factor), rounded(fold(vim) * factor), inverse, held, 4)
    send[...] = held[...].astype(BF16)


def repeats():
    row = lax.broadcasted_iota(jnp.int32, (128, C), 0)
    return jnp.where((row & 31) == lax.broadcasted_iota(jnp.int32, (128, C), 1), 1.0, 0.0)


def blocks(tall, picks):
    row = lax.broadcasted_iota(jnp.int32, (128, 128), 0)
    wide = nt(tall.astype(BF16), picks)
    return jnp.where((row >> 5) == block_of((128, 128)), wide, 0.0).astype(BF16)


def point_kernel(recv, field, cotangent, local, bias, ytab, send, delta, held, wide):
    held[...] = recv[...].astype(F32)
    same = repeats()
    bias4 = jnp.sum(same * bias[...], axis=1, keepdims=True)
    picks = same.astype(BF16)
    local4 = blocks(nt(picks, local[...]), picks)
    ones = jnp.ones((16, N), BF16)
    total = jnp.zeros((144, 128), F32)
    outs = []
    for k in range(4):
        z, h = k // 2, k % 2
        spectrum = jnp.concatenate(
            [held[pl.ds(4 * z + 2 * p + h, KY, stride=8), :] for p in range(2)], axis=0
        )
        left = jnp.concatenate([spectrum.T.astype(BF16), local4], axis=1)
        rows = field[4 * h : 4 * h + 4, z].reshape(128, N)
        cot = cotangent[4 * h : 4 * h + 4, z].reshape(128, N)
        for part in range(4):
            cols = slice(256 * part, 256 * (part + 1))
            right = jnp.concatenate([ytab[:, cols], rows[:, cols]], axis=0)
            pre = nn(left, right) + bias4
            sig = 0.5 * jnp.tanh(0.5 * pre) + 0.5
            slope = sig * (1.0 + pre * (1.0 - sig))
            delta[k, :, cols] = (cot[:, cols].astype(F32) * slope).astype(BF16)
    for k in range(4):
        z, h = k // 2, k % 2
        rows = field[4 * h : 4 * h + 4, z].reshape(128, N)
        out = nt(jnp.concatenate([ytab[...], rows, ones], axis=0), delta[k])
        outs.append((z, h, out[:128]))
        total = total + out[128:]
    bias_total = total[128:]
    block = block_of((32, 128))
    diag = jnp.zeros((32, 128), F32)
    for r in range(4):
        diag = diag + jnp.where(block == r, total[32 * r : 32 * (r + 1)], 0.0)
    held[0:32, :] = fold(diag)
    block = block_of((8, 128))
    flat = jnp.zeros((8, 128), F32)
    for q in range(4):
        flat = flat + jnp.where(block == q, held[pl.ds(q, 8, stride=4), :], 0.0)
    bias = fold(bias_total[0:8])[0:1]
    bias_1 = rounded(bias)
    bias_2 = rounded(bias - bias_1)
    bias_3 = bias - bias_1 - bias_2
    block = block_of((1, 128))
    pieces = jnp.where(
        block == 0, bias_1, jnp.where(block == 1, bias_2, jnp.where(block == 2, bias_3, 0.0))
    )
    for z, h, out in outs:
        for p in range(2):
            wide[pl.ds(10 * z + 2 * p + h, KY, stride=20), :] = out[KY * p : KY * (p + 1)]
    for z in range(2):
        lines = [flat[4 * z + k : 4 * z + k + 1] for k in range(4)]
        lines = lines + [pieces, jnp.zeros((1, 128), F32)]
        for k, line in enumerate(lines):
            wide[pl.ds(10 * z + 4 + k, KY, stride=20), :] = jnp.broadcast_to(line, (KY, 128))
    send[...] = wide[...].astype(BF16)


def back_kernel(recv, forward, first, kept, share, held):
    real, imag = x_forward(recv, forward, held, 10)
    factor = mode_weight()
    real = rounded(real * factor)
    imag = rounded(imag * factor)
    kept[:KX] = real
    kept[KX:] = imag
    share[:64] = first[...]
    share[64:128] = packed(real, imag)
    lines = [
        jnp.sum(held[pl.ds(4 + k, 128, stride=10), :], axis=0, keepdims=True) for k in range(5)
    ]
    total = jnp.concatenate(lines[:4], axis=0)
    bias = fold(lines[4])
    share[128:] = jnp.concatenate(
        [
            rounded(total),
            total - rounded(total),
            rounded(bias),
            bias - rounded(bias),
            jnp.zeros((6, 128), F32),
        ],
        axis=0,
    ).astype(BF16)


def adjoint_kernel(kept, weight, inverse, share, send, group, held, high, low):
    dre = kept[:KX]
    dim = kept[KX:]
    for t in range(8):
        cols = slice(128 * t, 128 * (t + 1))
        wre = weight[:, cols].astype(F32)
        wim = weight[:, 1024 + 128 * t : 1024 + 128 * (t + 1)].astype(F32)
        for k, term in ((0, dre * wre + dim * wim), (1, dim * wre - dre * wim)):
            top = term.astype(BF16)
            high[KX * k : KX * (k + 1), cols] = top
            low[KX * k : KX * (k + 1), cols] = (term - top.astype(F32)).astype(BF16)
    k = lax.broadcasted_iota(jnp.int32, (1024, 128), 0)
    lane = lax.broadcasted_iota(jnp.int32, (1024, 128), 1)
    gather = jnp.where((k >> 5) == (lane & 31), 1.0, 0.0).astype(BF16)
    back = rounded(nn(high[...], gather) + nn(low[...], gather))
    x_inverse(back[:KX], back[KX:], inverse, held, 4)
    send[...] = held[...].astype(BF16)
    group[...] = share[...]


def final_kernel(
    recv, delta, local, ytab, groups, field_grad, spectral_grad, local_grad, bias_grad,
    held, rows, out, tiles, out_local, out_bias, sems,
):
    held[...] = recv[...].astype(F32)
    picks = repeats().astype(BF16)
    local4 = blocks(nn(picks, local[...]), picks)
    copies = [
        pltpu.make_async_copy(rows, field_grad, sems.at[0]),
        pltpu.make_async_copy(out, spectral_grad, sems.at[1]),
        pltpu.make_async_copy(out_local, local_grad, sems.at[2]),
        pltpu.make_async_copy(out_bias, bias_grad, sems.at[3]),
    ]
    for k in range(4):
        z, h = k // 2, k % 2
        spectrum = jnp.concatenate(
            [held[pl.ds(4 * z + 2 * p + h, KY, stride=8), :] for p in range(2)], axis=0
        )
        left = jnp.concatenate([spectrum.T.astype(BF16), local4], axis=1)
        for part in range(4):
            cols = slice(256 * part, 256 * (part + 1))
            right = jnp.concatenate([ytab[:, cols], delta[k, :, cols]], axis=0)
            rows[4 * h : 4 * h + 4, z, :, cols] = nn(left, right).astype(BF16).reshape(4, 32, 256)
    copies[0].start()
    lane = lax.broadcasted_iota(jnp.int32, (128, 1024), 1)
    k = lax.broadcasted_iota(jnp.int32, (128, 1024), 0)
    start = 64 * lax.axis_index("core")
    expands = [
        jnp.where((lane >> 5) + (start + 32 * part) == k, 1.0, 0.0).astype(BF16)
        for part in range(2)
    ]
    compact = jnp.concatenate([groups[144 * g : 144 * g + 64] for g in range(8)], axis=0)
    block = block_of((64, 128)) - 2 * lax.axis_index("core")
    for g in range(8):
        second = groups[144 * g + 64 : 144 * g + 128].astype(F32)
        for part in range(2):
            tiles[64 * (8 * part + g) : 64 * (8 * part + g + 1)] = fold(
                jnp.where(block == part, second, 0.0)
            )
    for pair in range(4):
        wide = [nn(compact, expand[:, 256 * pair : 256 * (pair + 1)]) for expand in expands]
        for half in range(2):
            t = 2 * pair + half
            cols = slice(128 * half, 128 * (half + 1))
            real = jnp.zeros((64, 128), F32)
            imag = jnp.zeros((64, 128), F32)
            for g in range(8):
                ure = wide[0][64 * g : 64 * (g + 1), cols]
                uim = wide[1][64 * g : 64 * (g + 1), cols]
                dre = tiles[64 * g : 64 * (g + 1)]
                dim = tiles[512 + 64 * g : 512 + 64 * (g + 1)]
                real = real + (ure * dre + uim * dim)
                imag = imag + (ure * dim - uim * dre)
            out[:, 128 * t : 128 * (t + 1)] = real.astype(BF16)
            out[:, 1024 + 128 * t : 1024 + 128 * (t + 1)] = imag.astype(BF16)
    gscale = float((N * N * 8) ** -0.5)
    halves = []
    for c in range(2):
        total = jnp.zeros((16, 128), F32)
        for g in range(4):
            at = 144 * (2 * g + c) + 128
            total = total + groups[at : at + 16].astype(F32)
        halves.append(total)
    flat = jnp.concatenate([total[0:4] + total[4:8] for total in halves], axis=0) * gscale
    total = halves[0]
    for q in range(4):
        out_local[pl.ds(q, 8, stride=4), :] = flat[:, 32 * q : 32 * (q + 1)]
    out_bias[...] = ((total[8:9] + total[9:10]) * gscale)[:, :32]
    for copy in copies[1:]:
        copy.start()
    for copy in copies:
        copy.wait()


def run(kernel, operands, outs, scratch, name, specs=None, out_specs=None):
    specs = specs or [VM] * len(operands)
    out_specs = out_specs or [VM] * len(outs)
    operands = [
        pltpu.with_memory_space_constraint(operand, pltpu.HBM) if spec is HBM else operand
        for operand, spec in zip(operands, specs)
    ]
    return pl.pallas_call(
        kernel,
        out_shape=[
            (pltpu.HBM if spec is HBM else jax.ShapeDtypeStruct)(*out)
            for out, spec in zip(outs, out_specs)
        ],
        in_specs=specs,
        out_specs=out_specs,
        scratch_shapes=scratch,
        compiler_params=pltpu.CompilerParams(vmem_limit_bytes=16 * 1024 * 1024),
        cost_estimate=pl.CostEstimate(
            flops=COST.get(name, 200_000_000), bytes_accessed=1 << 20, transcendentals=0
        ),
        name=name,
    )(*operands)


def exchange(values, *shape):
    blocks = values.reshape((128,) + shape)
    return lax.all_to_all(blocks, GX, 0, 0, tiled=True).reshape(values.shape)


def local(field, cotangent, spectral_weight, local_weight, bias):
    ytab, forward, inverse = (jnp.asarray(table) for table in tables())
    slab = ((512, 128), BF16)
    slab_wide = ((1280, 128), BF16)
    held = pltpu.VMEM((512, 128), F32)
    held_wide = pltpu.VMEM((1280, 128), F32)
    quarters = pltpu.VMEM((4, 4, C, N), BF16)

    send, bias_row, local_near = run(
        y_kernel,
        (field, ytab, bias.reshape(1, C), local_weight),
        [slab, ((1, C), F32), ((C, C), BF16)],
        [held, quarters, pltpu.VMEM((128, N), BF16), pltpu.SemaphoreType.DMA((7,))],
        "y_forward",
        [HBM] * 4,
    )
    recv = exchange(send, 4, 128)
    weight = lax.all_gather(spectral_weight, "core", axis=0, tiled=True)
    send, first = run(
        mix_kernel,
        (recv, weight, forward, inverse),
        [slab, ((64, 128), BF16)],
        [held],
        "mix",
    )
    recv = exchange(send, 4, 128)
    send, delta = run(
        point_kernel,
        (recv, field, cotangent, local_near, bias_row, ytab),
        [slab_wide, ((4, 128, N), BF16)],
        [
            held,
            held_wide,
        ],
        "pointwise",
    )
    recv = exchange(send, 5, 2, 128)
    second, share = run(
        back_kernel,
        (recv, forward, first),
        [((2 * KX, 128), F32), ((144, 128), BF16)],
        [held_wide],
        "x_forward",
    )
    send, group = run(
        adjoint_kernel,
        (second, weight, inverse, share),
        [slab, ((144, 128), BF16)],
        [held, pltpu.VMEM((256, 1024), BF16), pltpu.VMEM((256, 1024), BF16)],
        "adjoint",
    )
    recv = exchange(send, 4, 128)
    group = lax.all_gather(group, "core", axis=0, tiled=True)
    for pairs in ([[0, 1], [2, 3]], [[0, 3], [1, 2]]):
        group = lax.all_gather(group, "gz", axis=0, tiled=True, axis_index_groups=pairs)
    field_grad, spectral_grad, local_grad, bias_grad = run(
        final_kernel,
        (recv, delta, local_near, ytab, group),
        [((8, 2, C, N), BF16), ((64, 2048), BF16), ((C, C), F32), ((1, C), F32)],
        [
            held,
            pltpu.VMEM((8, 2, C, N), BF16),
            pltpu.VMEM((64, 2048), BF16),
            pltpu.VMEM((1024, 128), F32),
            pltpu.VMEM((C, C), F32),
            pltpu.VMEM((1, C), F32),
            pltpu.SemaphoreType.DMA((4,)),
        ],
        "final",
        None,
        [HBM] * 4,
    )
    return field_grad, spectral_grad, local_grad, bias_grad.reshape(C)


def solution(mesh):
    fine = Mesh(mesh.devices.reshape(8, 8, 2, 4), GX + ("gz",))
    cells = P(GX, "gz", None, None)
    return jax.shard_map(
        local,
        mesh=fine,
        in_specs=(cells, cells, P(GX, None), P(), P()),
        out_specs=(cells, P(GX, None), P(), P()),
        check_vma=False,
    )
```
